256 devices in a mesh: dp: 4 (over y), ctx: 16 (over x, z_lo), tp: 4 (over z_hi, core).
Axes of the slice: x: 4, y: 4, z: 8 (z_hi: 2, z_lo: 4; z = z_hi * 4 + z_lo), core: 2. Of those that a mesh axis runs over, the one named last changes fastest.
Arguments:
- normed: bfloat16 [4, 2048, 4096], P('dp', 'ctx'), may hold values from -24 to 24
- w_qkv: bfloat16 [4096, 3072], P(('dp', 'ctx'), 'tp'), may hold values from -0.09765625 to 0.09765625
- w_out: bfloat16 [4096, 2048], P(('dp', 'ctx'), 'tp'), may hold values from -0.125 to 0.125
- block_order: int32 [32], replicated, may hold values from 0 to 31, each once
- d_out: bfloat16 [4, 2048, 4096], P('dp', 'ctx'), may hold values from -6 to 6
Outputs:
- attn_out: bfloat16 [4, 2048, 4096], P('dp', 'ctx', 'tp')
- d_normed: bfloat16 [4, 2048, 4096], P('dp', 'ctx', 'tp')
- d_w_qkv: bfloat16 [4096, 3072], P(('dp', 'ctx'), 'tp')
- d_w_out: bfloat16 [4096, 2048], P(('dp', 'ctx'), 'tp')
The draws below stay inside these ranges and needn't reach their ends.
Inputs may be any that keep to these rules, and one draw needn't show every extreme that they name: `block_order`: each number appears once.
All inputs are finite; a program needn't handle non-finite values.
Results may differ from the reference program's by a relative error of at most 0.035.
Values may be sent and summed in bfloat16 or wider, within the bound.
A program may use at most 128 MiB of HBM per device.

```python
import jax
import jax.numpy as jnp
from jax import lax

D = 4096
HD = 128
HEADS_DEV = 4
KV_DEV = 1
TOK_DEV = 128
SEQS = 4
LENGTH = 2048
QKV_COLS = 3072
O_COLS = 2048
N_CTX = 16
N_TP = 4


def draw_normed(key, part):
    key = jax.random.fold_in(key, 11)
    full_shape = (SEQS, LENGTH, D)
    values = jnp.clip(jax.random.normal(key, full_shape, jnp.float32), -5.0, 5.0)
    return values.astype(jnp.bfloat16)


def draw_w_qkv(key, part):
    key = jax.random.fold_in(key, 23)
    full_shape = (D, QKV_COLS)
    values = jnp.clip(jax.random.normal(key, full_shape, jnp.float32), -6.0, 6.0) * D ** (-0.5)
    return values.astype(jnp.bfloat16)


def raised(result, own_key, source, target, blocks, factor):
    owner, partner = [(jnp.arange(result.shape[axis_at]) // (result.shape[axis_at] // blocks)).reshape([-1 if axis == axis_at else 1 for axis in range(result.ndim)]) for axis_at in (source, target)]
    chosen = jax.random.permutation(own_key, blocks)[partner]
    strong = (owner == chosen) | (owner == (partner + blocks // 2) % blocks)
    return jnp.where(strong, factor * result, result)


def shard_levels(key, dims, shards, least, largest):
    gain = 1.0
    for axis_at, blocks in shards:
        heights = jax.random.uniform(jax.random.fold_in(jax.random.fold_in(key, 6), axis_at), (blocks,), jnp.float32, least / len(shards), largest / len(shards))
        gain = gain * jnp.repeat(jnp.exp(heights), dims[axis_at] // blocks).reshape((-1,) + (1,) * (len(dims) - 1 - axis_at))
    return gain


def centred(key, extent, width, bound, cuts=(), kind=jnp.bfloat16):
    entries = width * jax.random.normal(key, extent, jnp.float32)
    if cuts:
        entries = entries * shard_levels(key, extent, cuts, -0.22, 0.18)
    return jnp.clip(entries, -bound, bound).astype(kind)


def bell_draw_with(rng, dims, width, limit, cuts, heavy, kind=jnp.bfloat16):
    values = width * jax.random.normal(rng, dims, jnp.float32)
    if cuts:
        values = values * shard_levels(rng, dims, cuts, -0.22, 0.18)
    return jnp.clip(raised(values, jax.random.fold_in(rng, 3), *heavy), -limit, limit).astype(kind)


def setup_inputs(seed: int = 0) -> dict:
    streams_of = jax.random.split(jax.random.key(seed), 6)
    return {
        "normed": draw_normed(jax.random.fold_in(streams_of[5], 71), 0),
        "w_qkv": draw_w_qkv(jax.random.fold_in(streams_of[5], 71), 0),
        "w_out": centred(streams_of[2], (D, O_COLS), O_COLS ** -0.5, 0.125, ((0, 64), (1, 4))),
        "block_order": jax.random.permutation(streams_of[3], 2 * N_CTX).astype(jnp.int32),
        "d_out": bell_draw_with(streams_of[4], (SEQS, LENGTH, D), 1.0, 6.0, ((0, 4), (1, 16)), (1, 2, 16, 2.0)),
    }


rope_base = 500000.0
masked_score = -1.0e30


def stored_positions(order, row_ids, block_rows):
    owner = row_ids // block_rows
    matches = owner[:, None] == jnp.arange(order.shape[0], dtype=jnp.int32)[None, :]
    picked = jnp.sum(jnp.where(matches, order[None, :], 0), axis=1)
    return (picked * block_rows + row_ids % block_rows).astype(jnp.int32)


def rope_tables(positions, head_size):
    half_size = head_size // 2
    frequency = rope_base ** (-2.0 * jnp.arange(half_size, dtype=jnp.float32) / head_size)
    angles = positions.astype(jnp.float32)[:, None] * frequency[None, :]
    angles = jnp.concatenate([angles, angles], axis=1)
    return jnp.cos(angles), jnp.sin(angles)


def rotate_half(values):
    half_size = values.shape[-1] // 2
    return jnp.concatenate([-values[..., half_size:], values[..., :half_size]], axis=-1)


def apply_rope(values, cosine, sines, direction_sign):
    table_shape = (cosine.shape[0],) + (1,) * (values.ndim - 2) + (cosine.shape[1],)
    return values * cosine.reshape(table_shape) + direction_sign * rotate_half(values) * sines.reshape(table_shape)


def round_bfloat(values):
    return lax.optimization_barrier(values.astype(jnp.bfloat16)).astype(jnp.float32)


def reference(normed, w_qkv, w_out, block_order, d_out):
    block_rows = TOK_DEV // 2
    group_size = HEADS_DEV // KV_DEV
    q_width = HEADS_DEV * HD
    kv_width = KV_DEV * HD
    block_width = q_width + 2 * kv_width
    score_scale = HD ** -0.5
    positions = stored_positions(block_order, jnp.arange(LENGTH, dtype=jnp.int32), block_rows)
    cosine, sines = rope_tables(positions, HD)
    allowed = positions[None, :] <= positions[:, None]
    qkv_blocks = jnp.transpose(w_qkv.reshape(D, N_TP, block_width), (1, 0, 2))
    out_blocks = jnp.transpose(w_out.reshape(D, N_TP, q_width), (1, 0, 2))

    def one_group(tokens, upstream, qkv_weight, out_weight):
        projected = jnp.dot(tokens, qkv_weight, preferred_element_type=jnp.float32)
        queries = apply_rope(projected[:, :q_width].reshape(LENGTH, KV_DEV, group_size, HD), cosine, sines, 1.0).astype(jnp.bfloat16)
        key_rows = apply_rope(projected[:, q_width:q_width + kv_width].reshape(LENGTH, KV_DEV, HD), cosine, sines, 1.0).astype(jnp.bfloat16)
        value_rows = projected[:, q_width + kv_width:].reshape(LENGTH, KV_DEV, HD).astype(jnp.bfloat16)
        query_f = queries.astype(jnp.float32)
        key_f = key_rows.astype(jnp.float32)
        value_f = value_rows.astype(jnp.float32)
        scores = jnp.einsum("tkgd,skd->kgts", query_f, key_f) * score_scale
        scores = jnp.where(allowed, scores, masked_score)
        row_max = jnp.max(scores, axis=-1)
        raw = jnp.where(allowed, jnp.exp(scores - row_max[..., None]), 0.0)
        row_sum = jnp.sum(raw, axis=-1)
        attended = jnp.einsum("kgts,skd->kgtd", round_bfloat(raw), value_f) / row_sum[..., None]
        heads_out = jnp.transpose(attended, (2, 0, 1, 3)).reshape(LENGTH, q_width).astype(jnp.bfloat16)
        head_grads = jnp.dot(upstream, out_weight, preferred_element_type=jnp.float32).astype(jnp.bfloat16)
        grads_four = head_grads.reshape(LENGTH, KV_DEV, group_size, HD).astype(jnp.float32)
        out_four = heads_out.reshape(LENGTH, KV_DEV, group_size, HD).astype(jnp.float32)
        row_dots = jnp.einsum("tkgd,tkgd->kgt", grads_four, out_four)
        weights = raw / row_sum[..., None]
        dweights = jnp.einsum("tkgd,skd->kgts", grads_four, value_f)
        dscores = round_bfloat(weights * (dweights - row_dots[..., None]))
        query_grad = jnp.einsum("kgts,skd->tkgd", dscores, key_f) * score_scale
        key_grad = jnp.einsum("kgts,tkgd->skd", dscores, query_f) * score_scale
        value_grad = jnp.einsum("kgts,tkgd->skd", round_bfloat(weights), grads_four)
        query_pre = apply_rope(query_grad, cosine, sines, -1.0)
        key_pre = apply_rope(key_grad, cosine, sines, -1.0)
        qkv_grads = jnp.concatenate([query_pre.reshape(LENGTH, q_width), key_pre.reshape(LENGTH, kv_width), value_grad.reshape(LENGTH, kv_width)], axis=1).astype(jnp.bfloat16)
        return heads_out, qkv_grads

    def per_sequence(sequence):
        tokens, upstream = sequence

        def group_step(carry, pair):
            heads_out, qkv_grads = one_group(tokens, upstream, pair[0], pair[1])
            out_part = round_bfloat(jnp.dot(heads_out, pair[1].T, preferred_element_type=jnp.float32))
            in_part = round_bfloat(jnp.dot(qkv_grads, pair[0].T, preferred_element_type=jnp.float32))
            return (carry[0] + out_part, carry[1] + in_part), (heads_out, qkv_grads)

        zero_rows = jnp.zeros((LENGTH, D), jnp.float32)
        sums, per_group = lax.scan(group_step, (zero_rows, zero_rows), (qkv_blocks, out_blocks))
        return sums[0].astype(jnp.bfloat16), sums[1].astype(jnp.bfloat16), per_group[0], per_group[1]

    attn_out, d_normed, heads_all, grads_all = lax.map(per_sequence, (normed, d_out))
    heads_all = jnp.transpose(heads_all, (0, 2, 1, 3)).reshape(SEQS, LENGTH, O_COLS)
    grads_all = jnp.transpose(grads_all, (0, 2, 1, 3)).reshape(SEQS, LENGTH, QKV_COLS)

    def by_run(state, run_index):
        first_row = (run_index * TOK_DEV).astype(jnp.int32)
        qkv_sum = jnp.zeros((D, QKV_COLS), jnp.float32)
        out_sum = jnp.zeros((D, O_COLS), jnp.float32)
        for sequence in range(SEQS):
            tokens = lax.dynamic_slice_in_dim(normed[sequence], first_row, TOK_DEV, 0)
            upstream = lax.dynamic_slice_in_dim(d_out[sequence], first_row, TOK_DEV, 0)
            grads = lax.dynamic_slice_in_dim(grads_all[sequence], first_row, TOK_DEV, 0)
            heads = lax.dynamic_slice_in_dim(heads_all[sequence], first_row, TOK_DEV, 0)
            qkv_sum = qkv_sum + round_bfloat(jnp.dot(tokens.T, grads, preferred_element_type=jnp.float32))
            out_sum = out_sum + round_bfloat(jnp.dot(upstream.T, heads, preferred_element_type=jnp.float32))
        return (state[0] + round_bfloat(qkv_sum), state[1] + round_bfloat(out_sum)), None

    start_state = (jnp.zeros((D, QKV_COLS), jnp.float32), jnp.zeros((D, O_COLS), jnp.float32))
    totals, unused = lax.scan(by_run, start_state, jnp.arange(N_CTX, dtype=jnp.int32))
    return attn_out, d_normed, totals[0].astype(jnp.bfloat16), totals[1].astype(jnp.bfloat16)
```

```python
import jax
import jax.numpy as jnp
from jax import lax
from jax.experimental import pallas as pl
from jax.experimental.pallas import tpu as pltpu
from jax.sharding import PartitionSpec as P

HD = 128
SIDE = 4
MESH = pl.DeviceIdType.MESH

rope_base = 500000.0
masked_score = -1e30


def stored_positions(order, row_ids, block_rows):
    owner = row_ids // block_rows
    matches = owner[:, None] == jnp.arange(order.shape[0], dtype=jnp.int32)[None, :]
    picked = jnp.sum(jnp.where(matches, order[None, :], 0), axis=1)
    return picked * block_rows + row_ids % block_rows


def rope_tables(positions, head_size):
    half_size = head_size // 2
    frequency = rope_base ** (-2.0 * jnp.arange(half_size, dtype=jnp.float32) / head_size)
    angles = positions.astype(jnp.float32)[:, None] * frequency[None, :]
    angles = jnp.concatenate([angles, angles], axis=1)
    return (jnp.cos(angles), jnp.sin(angles))


def rotate_half(values):
    half_size = values.shape[-1] // 2
    return jnp.concatenate([-values[..., half_size:], values[..., :half_size]], axis=-1)


def apply_rope(values, cosine, sines, direction_sign):
    return values * cosine[:, None, :] + direction_sign * rotate_half(values) * sines[:, None, :]


class Links:
    def __init__(self, send, recv):
        self.send, self.recv, self.used, self.copies = send, recv, 0, []
        self.y = lax.axis_index("dp")
        self.c = lax.axis_index("ctx")
        self.t = lax.axis_index("tp")
        self.x = self.c // SIDE
        self.z = self.c % SIDE

    def along_y(self, k):
        return (lax.rem(self.y + k, SIDE), self.c, self.t)

    def along_x(self, k):
        return (self.y, lax.rem(self.x + k, SIDE) * SIDE + self.z, self.t)

    def along_z(self, k):
        return (self.y, self.x * SIDE + lax.rem(self.z + k, SIDE), self.t)

    def other_core(self):
        return (self.y, self.c, self.t + 1 - 2 * lax.rem(self.t, 2))

    def other_side(self):
        return (self.y, self.c, lax.rem(self.t + 2, 4))

    def greet(self, partners):
        barrier = pltpu.get_barrier_semaphore()
        for partner in partners:
            pl.semaphore_signal(barrier, inc=1, device_id=partner, device_id_type=MESH)
        pl.semaphore_wait(barrier, len(partners))

    def copy(self, source, target, partner):
        made = pltpu.make_async_remote_copy(
            src_ref=source,
            dst_ref=target,
            send_sem=self.send.at[self.used],
            recv_sem=self.recv.at[self.used],
            device_id=partner,
            device_id_type=MESH,
        )
        made.start()
        self.used += 1
        self.copies.append(made)
        return made

    def finish(self):
        for made in self.copies:
            made.wait_send()


def interleave(streams):
    streams = list(streams)
    while streams:
        left = []
        for stream in streams:
            try:
                next(stream)
                left.append(stream)
            except StopIteration:
                pass
        streams = left


def ring_gather(links, along, here, view):
    before, after = lax.rem(here + 3, SIDE), lax.rem(here + 1, SIDE)
    own = view(here, None)
    right = links.copy(own, own, along(1))
    left = links.copy(own, own, along(3))
    yield
    right.wait_recv()
    passed = view(before, 0)
    onward = links.copy(passed, passed, along(1))
    left.wait_recv()
    passed = view(after, 1)
    back = links.copy(passed, passed, along(3))
    yield
    onward.wait_recv()
    back.wait_recv()


def both(first, second):
    done = object()
    while True:
        a, b = next(first, done), next(second, done)
        if a is done and b is done:
            return
        yield


def line_gather(links, source, place, local_sem):
    local = pltpu.make_async_copy(source, place, local_sem)
    local.start()
    copies = [links.copy(source, place, links.along_z(k)) for k in (1, 3, 2)]
    yield
    for made in copies:
        made.wait_recv()
    local.wait()


def halves(index_of):
    def view(i, h):
        return index_of(i, slice(None) if h is None else pl.ds(2 * h, 2))

    return view


def gather_weight(links, source, full, local_sem):
    y, x, z = links.y, links.x, links.z
    yield from line_gather(links, source, full.at[y, x, z], local_sem)
    yield from both(
        ring_gather(links, links.along_x, x, halves(lambda i, part: full.at[y, i, part, 0])),
        ring_gather(links, links.along_y, y, halves(lambda i, part: full.at[i, x, part, 1])),
    )
    yield from both(
        ring_gather(links, links.along_y, y, halves(lambda i, part: full.at[i, part, :, 0])),
        ring_gather(links, links.along_x, x, halves(lambda i, part: full.at[part, i, :, 1])),
    )


def gather_weights_kernel(w_qkv, w_out, full_qkv, full_out, send, recv, local):
    links = Links(send, recv)
    links.greet(
        [links.along_z(k) for k in (1, 2, 3)]
        + [links.along_x(1), links.along_x(3), links.along_y(1), links.along_y(3)]
    )
    interleave(
        [
            gather_weight(links, w_qkv, full_qkv, local.at[0]),
            gather_weight(links, w_out, full_out, local.at[1]),
        ]
    )
    links.finish()


def gather_rows_kernel(rows, full, send, recv, local):
    links = Links(send, recv)
    links.greet([links.along_z(k) for k in (1, 2, 3)] + [links.along_x(1), links.along_x(3)])

    def stream():
        yield from line_gather(links, rows, full.at[links.x, links.z], local.at[0])
        yield from ring_gather(
            links, links.along_x, links.x, halves(lambda i, part: full.at[i, part])
        )

    interleave([stream()])
    links.finish()


def add_blocks(target, *terms):
    first, second = target.shape[0], target.shape[1]

    def step(i, carry):
        at = (i // second, i % second)
        total = terms[0][at].astype(jnp.float32)
        for term in terms[1:]:
            total = total + term[at].astype(jnp.float32)
        target[at] = total.astype(target.dtype)
        return carry

    lax.fori_loop(0, first * second, step, 0)


def ring_sum(links, along, here, view, result, scratch):
    passing, from_left, from_right = scratch
    left, right, across = (
        lax.rem(here + 3, SIDE),
        lax.rem(here + 1, SIDE),
        lax.rem(here + 2, SIDE),
    )
    first = links.copy(view(across, 0), passing.at[0], along(1))
    second = links.copy(view(across, 1), passing.at[1], along(3))
    plain_right = links.copy(view(right, 1), from_left.at[1], along(1))
    plain_left = links.copy(view(left, 0), from_right.at[0], along(3))
    yield
    first.wait_recv()
    add_blocks(passing.at[0], passing.at[0], view(right, 0))
    summed_right = links.copy(passing.at[0], from_left.at[0], along(1))
    second.wait_recv()
    add_blocks(passing.at[1], passing.at[1], view(left, 1))
    summed_left = links.copy(passing.at[1], from_right.at[1], along(3))
    yield
    plain_left.wait_recv()
    summed_right.wait_recv()
    add_blocks(result(0), view(here, 0), from_left.at[0], from_right.at[0])
    plain_right.wait_recv()
    summed_left.wait_recv()
    add_blocks(result(1), view(here, 1), from_left.at[1], from_right.at[1])


def line_sum(links, terms, result, arrived):
    copies = [
        links.copy(terms.at[lax.rem(links.z + k, SIDE)], arrived.at[k - 1], links.along_z(k))
        for k in (1, 3, 2)
    ]
    yield
    for made in copies:
        made.wait_recv()
    own = terms.at[links.z]
    rows = 32

    def step(i, carry):
        at = (i // (own.shape[1] // rows), pl.ds(i % (own.shape[1] // rows) * rows, rows))
        total = own[at].astype(jnp.float32)
        for k in range(3):
            total = total + arrived[(k,) + at].astype(jnp.float32)
        result[at] = total.astype(result.dtype)
        return carry

    lax.fori_loop(0, own.shape[0] * (own.shape[1] // rows), step, 0)


def sum_weight(links, terms, result, scratch):
    ring_ya, ring_xb, mid_a, mid_b, ring_xa, ring_yb, last, arrived = scratch
    y, x = links.y, links.x
    yield from both(
        ring_sum(
            links, links.along_y, y,
            lambda i, h: terms.at[i, pl.ds(2 * h, 2), :, 0],
            lambda h: mid_a.at[pl.ds(2 * h, 2)], ring_ya,
        ),
        ring_sum(
            links, links.along_x, x,
            lambda i, h: terms.at[pl.ds(2 * h, 2), i, :, 1],
            lambda h: mid_b.at[pl.ds(2 * h, 2)], ring_xb,
        ),
    )
    yield from both(
        ring_sum(
            links, links.along_x, x,
            lambda i, h: mid_a.at[pl.ds(i, 1), pl.ds(2 * h, 2)],
            lambda h: last.at[pl.ds(0, 1), pl.ds(2 * h, 2), 0], ring_xa,
        ),
        ring_sum(
            links, links.along_y, y,
            lambda i, h: mid_b.at[pl.ds(i, 1), pl.ds(2 * h, 2)],
            lambda h: last.at[pl.ds(0, 1), pl.ds(2 * h, 2), 1], ring_yb,
        ),
    )
    yield from line_sum(links, last.at[0], result, arrived)


def sum_weight_scratch(columns):
    def vmem(*shape):
        return pltpu.VMEM(shape + (32, columns), jnp.bfloat16)

    big = (vmem(2, 2, 4), vmem(2, 2, 4), vmem(2, 2, 4))
    small = (vmem(2, 1, 2), vmem(2, 1, 2), vmem(2, 1, 2))
    return (big, big, vmem(4, 4), vmem(4, 4), small, small, vmem(1, 4, 2), vmem(3, 2))


def sum_rows(links, terms, result, scratch):
    ring, middle, arrived = scratch
    yield from ring_sum(
        links, links.along_x, links.x,
        lambda i, h: terms.at[pl.ds(i, 1), pl.ds(2 * h, 2)],
        lambda h: middle.at[pl.ds(0, 1), pl.ds(2 * h, 2), 0], ring,
    )
    yield from line_sum(links, middle.at[0], result, arrived)


def sum_rows_scratch(rows, columns):
    def vmem(*shape):
        return pltpu.VMEM(shape + (rows, columns), jnp.bfloat16)

    small = (vmem(2, 1, 2), vmem(2, 1, 2), vmem(2, 1, 2))
    return (small, pltpu.VMEM((1, 4, 1, rows, columns), jnp.bfloat16), pltpu.VMEM((3, 1, rows, columns), jnp.bfloat16))


def sum_groups(links, terms, result, scratch):
    near, pair, far = scratch
    width = result.shape[1]
    core = lax.rem(links.t, 2)
    side = links.t // 2

    def columns(owner):
        return pl.ds(pl.multiple_of(owner * width, width), width)

    far_owner = (1 - side) * 2
    near_owner = side * 2
    first = links.copy(
        terms.at[:, columns(far_owner + 1 - core)], near.at[0], links.other_core()
    )
    second = links.copy(
        terms.at[:, columns(near_owner + 1 - core)], near.at[1], links.other_core()
    )
    yield
    first.wait_recv()
    rows = 16
    steps = result.shape[0] // rows

    def pair_step(i, carry):
        at = pl.ds(i * rows, rows)
        total = terms[at, columns(far_owner + core)].astype(jnp.float32) + near[0, at].astype(
            jnp.float32
        )
        pair[at] = total.astype(pair.dtype)
        return carry

    lax.fori_loop(0, steps, pair_step, 0)
    across = links.copy(pair, far, links.other_side())
    yield
    yield
    yield
    second.wait_recv()
    across.wait_recv()

    def last_step(i, carry):
        at = pl.ds(i * rows, rows)
        total = terms[at, columns(near_owner + core)].astype(jnp.float32) + near[1, at].astype(
            jnp.float32
        )
        result[at] = (total + far[at].astype(jnp.float32)).astype(result.dtype)
        return carry

    lax.fori_loop(0, steps, last_step, 0)


def sum_groups_scratch(rows, width):
    return (
        pltpu.VMEM((2, rows, width), jnp.bfloat16),
        pltpu.VMEM((rows, width), jnp.bfloat16),
        pltpu.VMEM((rows, width), jnp.bfloat16),
    )


def all_partners(links):
    return (
        [links.along_z(k) for k in (1, 2, 3)]
        + [links.along_x(1), links.along_x(3), links.along_y(1), links.along_y(3)]
        + [links.other_core(), links.other_side()]
    )


def middle_sums_kernel(kv_terms, group_terms, weight_terms, kv_sum, group_sum, weight_sum, scratch, send, recv):
    links = Links(send, recv)
    links.greet(all_partners(links))
    interleave(
        [
            sum_rows(links, kv_terms, kv_sum, scratch[0]),
            sum_groups(links, group_terms, group_sum, scratch[1]),
            sum_weight(links, weight_terms, weight_sum, scratch[2]),
        ]
    )
    links.finish()


def last_sums_kernel(group_terms, weight_terms, group_sum, weight_sum, scratch, send, recv):
    links = Links(send, recv)
    links.greet(all_partners(links))
    interleave(
        [
            sum_groups(links, group_terms, group_sum, scratch[0]),
            sum_weight(links, weight_terms, weight_sum, scratch[1]),
        ]
    )
    links.finish()


def attention_kernel(query_pos, key_pos, queries, head_grads, kv, heads_out, query_grad, kv_grad, totals):
    score_scale = HD ** (-0.5)
    keys, values = kv[:, :HD], kv[:, HD:]
    keys_t, values_t = keys.T, values.T
    rows = 256
    last = (((1,), (1,)), ((), ()))
    totals[...] = jnp.zeros_like(totals)

    def step(i, carry):
        at = pl.ds(i * rows, rows)
        q, grads = queries[at], head_grads[at]
        allowed = key_pos[...] <= query_pos[...]
        scores = lax.dot_general(keys, q, last, preferred_element_type=jnp.float32) * score_scale
        scores = jnp.where(allowed, scores, masked_score)
        row_max = jnp.max(scores, axis=0, keepdims=True)
        raw = jnp.where(allowed, jnp.exp(scores - row_max), 0.0)
        row_sum = jnp.sum(raw, axis=0, keepdims=True)
        weighted = jnp.dot(values_t, raw.astype(jnp.bfloat16), preferred_element_type=jnp.float32)
        out = (weighted / row_sum).astype(jnp.bfloat16)
        out_rows = out.astype(jnp.float32).T
        row_dots = jnp.sum(grads.astype(jnp.float32).T * out.astype(jnp.float32), axis=0, keepdims=True)
        weights = raw * (1.0 / row_sum)
        dweights = lax.dot_general(values, grads, last, preferred_element_type=jnp.float32)
        dscores = (weights * (dweights - row_dots)).astype(jnp.bfloat16)
        heads_out[at] = out_rows.astype(jnp.bfloat16)
        dq = jnp.dot(keys_t, dscores, preferred_element_type=jnp.float32)
        query_grad[at] = dq.T * score_scale
        totals[:, :HD] += jnp.dot(dscores, q, preferred_element_type=jnp.float32) * score_scale
        totals[:, HD:] += jnp.dot(weights.astype(jnp.bfloat16), grads, preferred_element_type=jnp.float32)
        return carry

    lax.fori_loop(0, queries.shape[0] // rows, step, 0)
    kv_grad[...] = totals[...].astype(jnp.bfloat16)


VMEM = pl.BlockSpec(memory_space=pltpu.VMEM)
HBM = pl.BlockSpec(memory_space=pl.ANY)


def call(kernel, outs, ins, in_specs, out_specs, scratch, identity=None, copies=0, limit=40):
    if copies:
        scratch = list(scratch) + [pltpu.SemaphoreType.DMA((copies,))] * 2
    return pl.pallas_call(
        kernel,
        out_shape=outs,
        in_specs=in_specs,
        out_specs=out_specs,
        scratch_shapes=scratch,
        compiler_params=pltpu.CompilerParams(
            collective_id=identity,
            has_side_effects=identity is not None,
            vmem_limit_bytes=limit * 2**20,
        ),
    )(*ins)


def shape(dims, kind=jnp.bfloat16):
    return jax.ShapeDtypeStruct(dims, kind)


def body(normed, w_qkv, w_out, block_order, d_out):
    local_rows = normed.shape[1]
    block_rows = local_rows // 2
    model = normed.shape[2]
    q_width = w_out.shape[1]
    qkv_width = w_qkv.shape[1]
    head_count = q_width // HD
    ctx_count = lax.axis_size("ctx")
    length = local_rows * ctx_count
    ctx_index = lax.axis_index("ctx")
    query_pos = stored_positions(
        block_order, ctx_index * local_rows + jnp.arange(local_rows, dtype=jnp.int32), block_rows
    )
    all_pos = stored_positions(block_order, jnp.arange(length, dtype=jnp.int32), block_rows)

    full_qkv, full_out = pl.pallas_call(
        gather_weights_kernel,
        out_shape=[shape((4, 4, 4, 2, 32, qkv_width)), shape((4, 4, 4, 2, 32, q_width))],
        in_specs=[HBM, HBM],
        out_specs=[HBM, HBM],
        scratch_shapes=[
            pltpu.SemaphoreType.DMA((38,)),
            pltpu.SemaphoreType.DMA((38,)),
            pltpu.SemaphoreType.DMA((2,)),
        ],
        compiler_params=pltpu.CompilerParams(collective_id=1, has_side_effects=True),
    )(w_qkv.reshape(2, 32, qkv_width), w_out.reshape(2, 32, q_width))
    qkv_weight = full_qkv.reshape(model, qkv_width)
    out_weight = full_out.reshape(model, q_width)

    tokens = normed[0]
    upstream = d_out[0]
    projected = jnp.dot(tokens, qkv_weight, preferred_element_type=jnp.float32)
    cosine, sines = rope_tables(query_pos, HD)
    turned = apply_rope(
        projected[:, : q_width + HD].reshape(local_rows, head_count + 1, HD), cosine, sines, 1.0
    ).astype(jnp.bfloat16)
    kv = jnp.concatenate(
        [turned[:, head_count], projected[:, q_width + HD :].astype(jnp.bfloat16)], axis=1
    )
    full_kv = pl.pallas_call(
        gather_rows_kernel,
        out_shape=shape((4, 4, local_rows, 2 * HD)),
        in_specs=[HBM],
        out_specs=HBM,
        scratch_shapes=[
            pltpu.SemaphoreType.DMA((7,)),
            pltpu.SemaphoreType.DMA((7,)),
            pltpu.SemaphoreType.DMA((1,)),
        ],
        compiler_params=pltpu.CompilerParams(collective_id=2, has_side_effects=True),
    )(kv).reshape(length, 2 * HD)

    head_grads = jnp.dot(upstream, out_weight, preferred_element_type=jnp.float32).astype(
        jnp.bfloat16
    )

    def by_head(rows):
        return jnp.transpose(rows.reshape(local_rows, head_count, HD), (1, 0, 2)).reshape(
            head_count * local_rows, HD
        )

    def by_row(heads):
        return jnp.transpose(heads.reshape(head_count, local_rows, HD), (1, 0, 2)).reshape(
            local_rows, q_width
        )

    stacked = head_count * local_rows
    heads_out, query_grad, kv_terms = call(
        attention_kernel,
        [
            shape((stacked, HD)),
            shape((stacked, HD), jnp.float32),
            shape((length, 2 * HD)),
        ],
        [
            jnp.concatenate([query_pos, query_pos])[None, :],
            all_pos[:, None],
            by_head(turned[:, :head_count].reshape(local_rows, q_width)),
            by_head(head_grads),
            full_kv,
        ],
        [VMEM] * 5,
        [VMEM] * 3,
        [pltpu.VMEM((length, 2 * HD), jnp.float32)],
    )
    heads_out = by_row(heads_out)
    out_term = lax.dot_general(
        heads_out, out_weight, (((1,), (1,)), ((), ())), preferred_element_type=jnp.float32
    ).astype(jnp.bfloat16)
    out_weight_term = lax.dot_general(
        upstream, heads_out, (((0,), (0,)), ((), ())), preferred_element_type=jnp.float32
    ).astype(jnp.bfloat16)
    width = model // 4
    kv_sum, attn_out, d_w_out = call(
        middle_sums_kernel,
        [
            shape((1, local_rows, 2 * HD), jnp.float32),
            shape((local_rows, width)),
            shape((2, 32, q_width)),
        ],
        [
            kv_terms.reshape(4, 4, local_rows, 2 * HD),
            out_term,
            out_weight_term.reshape(4, 4, 4, 2, 32, q_width),
        ],
        [VMEM] * 3,
        [VMEM] * 3,
        [
            (
                sum_rows_scratch(local_rows, 2 * HD),
                sum_groups_scratch(local_rows, width),
                sum_weight_scratch(q_width),
            )
        ],
        identity=3,
        copies=9 + 3 + 27,
    )
    rotated = apply_rope(
        jnp.concatenate([by_row(query_grad), kv_sum[0, :, :HD]], axis=1).reshape(
            local_rows, head_count + 1, HD
        ),
        cosine,
        sines,
        -1.0,
    )
    qkv_grads = jnp.concatenate(
        [rotated.reshape(local_rows, q_width + HD), kv_sum[0, :, HD:]], axis=1
    ).astype(jnp.bfloat16)
    input_term = lax.dot_general(
        qkv_grads, qkv_weight, (((1,), (1,)), ((), ())), preferred_element_type=jnp.float32
    ).astype(jnp.bfloat16)
    qkv_weight_term = lax.dot_general(
        tokens, qkv_grads, (((0,), (0,)), ((), ())), preferred_element_type=jnp.float32
    ).astype(jnp.bfloat16)
    d_normed, d_w_qkv = call(
        last_sums_kernel,
        [shape((local_rows, width)), shape((2, 32, qkv_width))],
        [input_term, qkv_weight_term.reshape(4, 4, 4, 2, 32, qkv_width)],
        [VMEM] * 2,
        [VMEM] * 2,
        [(sum_groups_scratch(local_rows, width), sum_weight_scratch(qkv_width))],
        identity=4,
        copies=3 + 27,
    )
    return (
        attn_out[None],
        d_normed[None],
        d_w_qkv.reshape(w_qkv.shape),
        d_w_out.reshape(w_out.shape),
    )


def solution(mesh):
    in_specs = (
        P("dp", "ctx", None),
        P(("dp", "ctx"), "tp"),
        P(("dp", "ctx"), "tp"),
        P(),
        P("dp", "ctx", None),
    )
    out_specs = (
        P("dp", "ctx", "tp"),
        P("dp", "ctx", "tp"),
        P(("dp", "ctx"), "tp"),
        P(("dp", "ctx"), "tp"),
    )
    return jax.shard_map(body, mesh=mesh, in_specs=in_specs, out_specs=out_specs, check_vma=False)
```

```python
import jax
import jax.numpy as jnp
from jax import lax
from jax.experimental import pallas as pl
from jax.experimental.pallas import tpu as pltpu
from jax.sharding import PartitionSpec as P

HD = 128
SIDE = 4
MESH = pl.DeviceIdType.MESH

rope_base = 500000.0
masked_score = -1e30
contract_last = (((1,), (1,)), ((), ()))
contract_first = (((0,), (0,)), ((), ()))


def stored_positions(order, row_ids, block_rows):
    owner = row_ids // block_rows
    matches = owner[:, None] == jnp.arange(order.shape[0], dtype=jnp.int32)[None, :]
    picked = jnp.sum(jnp.where(matches, order[None, :], 0), axis=1)
    return picked * block_rows + row_ids % block_rows


def rope_tables(positions, head_size):
    half_size = head_size // 2
    frequency = rope_base ** (-2.0 * jnp.arange(half_size, dtype=jnp.float32) / head_size)
    angles = positions.astype(jnp.float32)[:, None] * frequency[None, :]
    sines = jnp.sin(angles)
    cosine = jnp.cos(angles)
    return (
        jnp.concatenate([cosine, cosine], axis=1),
        jnp.concatenate([-sines, sines], axis=1),
    )


def swap_halves(values):
    half_size = values.shape[-1] // 2
    return jnp.concatenate([values[..., half_size:], values[..., :half_size]], axis=-1)


class Links:
    def __init__(self, send, recv):
        self.send, self.recv, self.used, self.copies = send, recv, 0, []
        self.y = lax.axis_index("dp")
        self.c = lax.axis_index("ctx")
        self.t = lax.axis_index("tp")
        self.x = self.c // SIDE
        self.z = self.c % SIDE
        self.core = lax.rem(self.t, 2)
        self.side = self.t // 2

    def along_y(self, k):
        return (lax.rem(self.y + k, SIDE), self.c, self.t)

    def along_x(self, k):
        return (self.y, lax.rem(self.x + k, SIDE) * SIDE + self.z, self.t)

    def along_z(self, k):
        return (self.y, self.x * SIDE + lax.rem(self.z + k, SIDE), self.t)

    def other_core(self):
        return (self.y, self.c, self.t + 1 - 2 * self.core)

    def other_side(self):
        return (self.y, self.c, lax.rem(self.t + 2, 4))

    def greet(self, sides=False):
        partners = (
            [self.along_y(k) for k in (1, 2, 3)]
            + [self.along_z(k) for k in (1, 2, 3)]
            + [self.along_x(1), self.along_x(3), self.other_core()]
        )
        if sides:
            partners.append(self.other_side())
        barrier = pltpu.get_barrier_semaphore()
        for partner in partners:
            pl.semaphore_signal(barrier, inc=1, device_id=partner, device_id_type=MESH)
        pl.semaphore_wait(barrier, len(partners))

    def copy(self, source, target, partner):
        made = pltpu.make_async_remote_copy(
            src_ref=source,
            dst_ref=target,
            send_sem=self.send.at[self.used],
            recv_sem=self.recv.at[self.used],
            device_id=partner,
            device_id_type=MESH,
        )
        made.start()
        self.used += 1
        self.copies.append(made)
        return made

    def finish(self):
        for made in self.copies:
            made.wait_send()


def local_copy(source, target, semaphore):
    made = pltpu.make_async_copy(source, target, semaphore)
    made.start()
    return made


def in_order(streams, order):
    for name in order:
        next(streams[name], None)
    for stream in streams.values():
        for _ in stream:
            pass


def column(i, width=HD):
    return pl.ds(pl.multiple_of(i * width, width), width)


def ring_gather(links, along, here, view, source=None, arrived=None):
    before, after, across = (
        lax.rem(here + 3, SIDE),
        lax.rem(here + 1, SIDE),
        lax.rem(here + 2, SIDE),
    )
    arrived = arrived or (lambda block: None)
    own = view(here, None)
    source = own if source is None else source
    right = links.copy(source, own, along(1))
    left = links.copy(source, own, along(3))
    yield
    right.wait_recv()
    passed = view(before, 0)
    onward = links.copy(passed, passed, along(1))
    left.wait_recv()
    passed = view(after, 1)
    back = links.copy(passed, passed, along(3))
    arrived(view(before, None))
    arrived(view(after, None))
    yield
    onward.wait_recv()
    arrived(view(across, 0))
    back.wait_recv()
    arrived(view(across, 1))


def gather_columns(links, source, chosen, full):
    y, x, z = links.y, links.x, links.z
    place = full.at[y, x, z]
    copies = [
        links.copy(source.at[:, column(chosen(lax.rem(y + k, SIDE)))], place, links.along_y(k))
        for k in (2, 1, 3)
    ]
    yield
    for made in copies:
        made.wait_recv()
    block = full.at[:, x, z]
    copies = [links.copy(block, block, links.along_z(k)) for k in (2, 1, 3)]
    yield
    for made in copies:
        made.wait_recv()
    yield from ring_gather(
        links,
        links.along_x,
        x,
        lambda i, h: full.at[:, i] if h is None else full.at[pl.ds(2 * h, 2), i],
    )


def gather_tokens(links, source, full):
    half = source.shape[0] // 2
    first = pl.multiple_of(links.core * half, half)
    handed = []

    def view(i, h):
        if h is None:
            return full.at[i, pl.ds(first, half)]
        return full.at[i, pl.ds(pl.multiple_of(first + h * (half // 2), half // 2), half // 2)]

    def hand(block):
        handed.append(links.copy(block, block, links.other_core()))

    yield from ring_gather(
        links, links.along_y, links.y, view, source.at[pl.ds(first, half)], hand
    )
    yield
    for made in handed:
        made.wait_recv()


def front_kernel(
    normed, d_out, w_qkv, w_out, all_normed, all_d_out, full_q, full_kv, full_out, held,
    send, recv, local,
):
    links = Links(send, recv)
    y, x, z = links.y, links.x, links.z
    heads = w_out.shape[1] // HD
    weights = {
        "q": (w_qkv, lambda j: j, full_q),
        "k": (w_qkv, lambda j: heads + lax.rem(j, 2), full_kv),
        "o": (w_out, lambda j: j, full_out),
    }
    mine = [
        local_copy(source.at[:, column(chosen(y))], full.at[y, x, z], local.at[i])
        for i, (source, chosen, full) in enumerate(weights.values())
    ]
    loads = [
        local_copy(source, held.at[i], local.at[3 + i]) for i, source in enumerate((normed, d_out))
    ]
    links.greet()
    for made in mine + loads:
        made.wait()
    streams = {name: gather_columns(links, *given) for name, given in weights.items()}
    streams["n"] = gather_tokens(links, held.at[0], all_normed)
    streams["d"] = gather_tokens(links, held.at[1], all_d_out)
    start = "qkon"
    for name in start:
        next(streams[name])
    kept = [
        local_copy(held.at[i], full.at[y], local.at[3 + i])
        for i, full in enumerate((all_normed, all_d_out))
    ]
    in_order(streams, "qkoqndknoqkdoqkdond")
    for made in kept:
        made.wait()
    links.finish()


def exchange_heads(links, source, place, own_semaphore):
    copies = [
        links.copy(source.at[lax.rem(links.y + k, SIDE)], place, links.along_y(k))
        for k in (2, 1, 3)
    ]
    return copies, local_copy(source.at[links.y], place, own_semaphore)


def middle_kernel(queries, grads, kv, all_queries, all_grads, all_kv, send, recv, local):
    links = Links(send, recv)
    y, x, z = links.y, links.x, links.z
    links.greet()
    place = all_kv.at[lax.rem(y, 2), x, z]
    passed = links.copy(kv.at[1], place, links.along_y(1))
    own = local_copy(kv.at[0], place, local.at[0])
    copies, mine = exchange_heads(links, queries, all_queries.at[y], local.at[1])
    more_copies, more_mine = exchange_heads(links, grads, all_grads.at[y], local.at[2])
    own.wait()
    passed.wait_recv()
    block = all_kv.at[:, x, z]
    for made in [links.copy(block, block, links.along_z(k)) for k in (2, 1, 3)]:
        made.wait_recv()
    for _ in ring_gather(
        links,
        links.along_x,
        x,
        lambda i, h: all_kv.at[:, i] if h is None else all_kv.at[pl.ds(h, 1), i],
    ):
        pass
    for made in copies + more_copies:
        made.wait_recv()
    mine.wait()
    more_mine.wait()
    links.finish()


def add_blocks(target, *terms):
    lead, (height, width) = target.shape[:-2], target.shape[-2:]
    rows = min(height, max(16, 16384 // width))
    per = height // rows
    count = per
    for size in lead:
        count *= size

    def step(i, carry):
        at = (pl.ds(pl.multiple_of(i % per * rows, rows), rows),)
        rest = i // per
        for size in lead[::-1]:
            at = (rest % size,) + at
            rest = rest // size
        total = terms[0][at].astype(jnp.float32)
        for term in terms[1:]:
            total = total + term[at].astype(jnp.float32)
        target[at] = total.astype(target.dtype)
        return carry

    lax.fori_loop(0, count, step, 0)


def ring_sum(links, along, here, view, result, scratch, prepare=None):
    passing, from_left, from_right = scratch
    left, right, across = (
        lax.rem(here + 3, SIDE),
        lax.rem(here + 1, SIDE),
        lax.rem(here + 2, SIDE),
    )
    prepare = prepare or (lambda i: None)
    prepare(across)
    first = links.copy(view(across, 0), passing.at[0], along(1))
    second = links.copy(view(across, 1), passing.at[1], along(3))
    prepare(right)
    plain_right = links.copy(view(right, 1), from_left.at[1], along(1))
    prepare(left)
    plain_left = links.copy(view(left, 0), from_right.at[0], along(3))
    yield
    prepare(here)
    first.wait_recv()
    add_blocks(passing.at[0], passing.at[0], view(right, 0))
    summed_right = links.copy(passing.at[0], from_left.at[0], along(1))
    second.wait_recv()
    add_blocks(passing.at[1], passing.at[1], view(left, 1))
    summed_left = links.copy(passing.at[1], from_right.at[1], along(3))
    yield
    plain_left.wait_recv()
    summed_right.wait_recv()
    add_blocks(result(0), view(here, 0), from_left.at[0], from_right.at[0])
    plain_right.wait_recv()
    summed_left.wait_recv()
    add_blocks(result(1), view(here, 1), from_left.at[1], from_right.at[1])


def sum_weight(links, tokens, grads, scratch):
    terms, ring, middle, arrived, summed, placed = scratch
    y, x, z = links.y, links.x, links.z
    size = 4 * terms.shape[3]

    def prepare(i):
        def step(owner, carry):
            at = column(owner * SIDE + i, size)
            rows = tokens[:, :, at].reshape(-1, size)
            part = lax.dot_general(
                rows,
                grads[...].reshape(rows.shape[0], HD),
                contract_first,
                preferred_element_type=jnp.float32,
            )
            terms[owner, i] = part.astype(jnp.bfloat16).reshape(terms.shape[2:])
            return carry

        lax.fori_loop(0, SIDE, step, 0)

    yield from ring_sum(
        links,
        links.along_x,
        x,
        lambda i, h: terms.at[pl.ds(2 * h, 2), i],
        lambda h: middle.at[pl.ds(2 * h, 2)],
        ring,
        prepare,
    )
    copies = [
        links.copy(middle.at[:, lax.rem(z + k, SIDE)], arrived.at[k - 1], links.along_z(k))
        for k in (2, 1, 3)
    ]
    yield
    for made in copies:
        made.wait_recv()
    add_blocks(summed, middle.at[:, z], arrived.at[0], arrived.at[1], arrived.at[2])
    copies = [
        links.copy(summed.at[lax.rem(y + k, SIDE)], placed.at[y], links.along_y(k))
        for k in (2, 1, 3)
    ]
    placed[y] = summed[y]
    yield
    for made in copies:
        made.wait_recv()


def sum_weight_scratch(rows):
    def vmem(*dims):
        return pltpu.VMEM(dims + (rows, HD), jnp.bfloat16)

    ring = (vmem(2, 2, 4), vmem(2, 2, 4), vmem(2, 2, 4))
    return (vmem(4, 4, 4), ring, vmem(4, 4), vmem(3, 4), vmem(4), vmem(4))


def sum_groups(links, rows, weight, result, scratch):
    terms, near, ring, paired, far = scratch
    width = result.shape[1]
    core, side = links.core, links.side
    size = 256

    def prepare(owner):
        def step(i, carry):
            part = lax.dot_general(
                rows[...].reshape(-1, rows.shape[2]),
                weight[pl.ds(pl.multiple_of(owner * width + i * size, size), size)],
                contract_last,
                preferred_element_type=jnp.float32,
            )
            terms[owner, :, :, column(i, size)] = part.astype(jnp.bfloat16).reshape(
                SIDE, rows.shape[1], size
            )
            return carry

        lax.fori_loop(0, width // size, step, 0)

    handed = []
    for i in range(2):
        prepare(2 * i + 1 - core)
        handed.append(links.copy(terms.at[2 * i + 1 - core], near.at[i], links.other_core()))
    for i in range(2):
        prepare(2 * i + core)
    yield
    for i in range(2):
        handed[i].wait_recv()
        add_blocks(terms.at[2 * i + core], terms.at[2 * i + core], near.at[i])
    yield from ring_sum(
        links,
        links.along_y,
        links.y,
        lambda i, h: terms.at[2 * h + core, i],
        lambda h: paired.at[h],
        ring,
    )
    across = links.copy(paired.at[1 - side], far, links.other_side())
    yield
    yield
    across.wait_recv()
    add_blocks(result, paired.at[side], far)


def sum_groups_scratch(rows, width):
    def vmem(*dims):
        return pltpu.VMEM(dims + (rows, width), jnp.bfloat16)

    return (vmem(4, 4), vmem(2, 4), (vmem(2), vmem(2), vmem(2)), vmem(2), vmem())


def sum_kv(links, terms, cosine, sines, grads, scratch):
    ring, middle, arrived, handed = scratch
    y, x, z = links.y, links.x, links.z
    yield from ring_sum(
        links,
        links.along_x,
        x,
        lambda i, h: terms.at[pl.ds(h, 1), i],
        lambda h: middle.at[pl.ds(h, 1)],
        ring,
    )
    copies = [
        links.copy(middle.at[:, lax.rem(z + k, SIDE)], arrived.at[k - 1], links.along_z(k))
        for k in (2, 1, 3)
    ]
    yield
    for made in copies:
        made.wait_recv()

    def total(kind):
        value = middle[kind, z].astype(jnp.float32)
        for k in range(3):
            value = value + arrived[k, kind].astype(jnp.float32)
        return value

    key, value = total(0), total(1)
    key = key * cosine[...] - pltpu.roll(key, HD // 2, 1) * sines[...]
    keeps_key = lax.rem(y, 2) == 0
    handed[...] = jnp.where(keeps_key, value, key).astype(jnp.bfloat16)
    passed = links.copy(handed, grads.at[y, :, pl.ds(HD, HD)], links.along_y(3))
    grads[y, :, HD:] = jnp.where(keeps_key, key, value).astype(jnp.bfloat16)
    yield
    passed.wait_recv()


def sum_kv_scratch(rows):
    def vmem(*dims):
        return pltpu.VMEM(dims + (rows, HD), jnp.bfloat16)

    return ((vmem(2, 1, 4), vmem(2, 1, 4), vmem(2, 1, 4)), vmem(2, 4), vmem(3, 2), vmem())


def back_kernel(
    heads_out, query_grad, kv_terms, cosine, sines, all_normed, all_d_out, full_q, full_kv, full_out,
    attn_out, d_normed, d_w_qkv, d_w_out,
    scratch, loaded, heads, grads, send, recv, local,
):
    links = Links(send, recv)
    y = links.y
    normed, d_out, w_qkv, w_out = loaded
    loads = [
        local_copy(source, target, local.at[i])
        for i, (source, target) in enumerate(
            [
                (full_out, w_out),
                (all_d_out, d_out),
                (all_normed, normed),
                (full_q, w_qkv.at[:, pl.ds(0, HD)]),
                (full_kv, w_qkv.at[:, pl.ds(HD, HD)]),
            ]
        )
    ]
    for k in (2, 3):
        grads[lax.rem(y + k, SIDE), :, HD:] = jnp.zeros_like(grads[0, :, HD:])
    links.greet(sides=True)

    kv_stream = sum_kv(links, kv_terms, cosine, sines, grads, scratch[0])
    next(kv_stream)
    head_copies, head_mine = exchange_heads(links, heads_out, heads.at[y], local.at[5])
    grad_copies, grad_mine = exchange_heads(
        links, query_grad, grads.at[y, :, pl.ds(0, HD)], local.at[6]
    )

    def keys_part():
        yield from kv_stream
        yield from sum_weight(links, normed, grads.at[:, :, pl.ds(HD, HD)], scratch[5])

    def queries_part():
        for made in grad_copies:
            made.wait_recv()
        grad_mine.wait()
        for made in loads[2:]:
            made.wait()
        yield from sum_weight(links, normed, grads.at[:, :, pl.ds(0, HD)], scratch[4])

    for made in head_copies:
        made.wait_recv()
    head_mine.wait()
    loads[0].wait()
    loads[1].wait()
    streams = {
        "a": sum_groups(links, heads, w_out, attn_out, scratch[1]),
        "k": keys_part(),
        "o": sum_weight(links, d_out, heads, scratch[3]),
        "q": queries_part(),
        "n": sum_groups(links, grads, w_qkv, d_normed, scratch[2]),
    }
    in_order(streams, "akokaqkoknaqnokaqnkonaqknoan")
    links.finish()
    placed_out, placed_q, placed_kv = scratch[3][5], scratch[4][5], scratch[5][5]
    width = SIDE * HD
    for j in range(SIDE):
        d_w_out[:, j * HD : (j + 1) * HD] = placed_out[j]
        d_w_qkv[:, j * HD : (j + 1) * HD] = placed_q[j]
    for kind in range(2):
        total = placed_kv[kind].astype(jnp.float32) + placed_kv[kind + 2].astype(jnp.float32)
        d_w_qkv[:, width + kind * HD : width + (kind + 1) * HD] = total.astype(jnp.bfloat16)


def attention_kernel(
    query_pos, key_pos, cosine, sines, queries, head_grads, kv, heads_out, query_grad, kv_grad, totals
):
    score_scale = HD ** (-0.5)
    keys, values = kv[0], kv[1]
    keys_t, values_t = keys.T, values.T
    rows = 256
    totals[...] = jnp.zeros_like(totals)

    def step(i, carry):
        at = pl.ds(pl.multiple_of(i * rows, rows), rows)
        q, grads = queries[at], head_grads[at]
        allowed = key_pos[...] <= query_pos[...]
        scores = (
            lax.dot_general(keys, q, contract_last, preferred_element_type=jnp.float32) * score_scale
        )
        scores = jnp.where(allowed, scores, masked_score)
        row_max = jnp.max(scores, axis=0, keepdims=True)
        raw = jnp.where(allowed, jnp.exp(scores - row_max), 0.0)
        row_sum = jnp.sum(raw, axis=0, keepdims=True)
        weighted = jnp.dot(values_t, raw.astype(jnp.bfloat16), preferred_element_type=jnp.float32)
        out = (weighted / row_sum).astype(jnp.bfloat16).astype(jnp.float32)
        row_dots = jnp.sum(grads.astype(jnp.float32).T * out, axis=0, keepdims=True)
        weights = raw * (1.0 / row_sum)
        dweights = lax.dot_general(values, grads, contract_last, preferred_element_type=jnp.float32)
        dscores = (weights * (dweights - row_dots)).astype(jnp.bfloat16)
        heads_out[at] = out.T.astype(jnp.bfloat16)
        dq = jnp.dot(keys_t, dscores, preferred_element_type=jnp.float32).T * score_scale
        dq = dq * cosine[...] - pltpu.roll(dq, HD // 2, 1) * sines[...]
        query_grad[at] = dq.astype(jnp.bfloat16)
        totals[0] += jnp.dot(dscores, q, preferred_element_type=jnp.float32) * score_scale
        totals[1] += jnp.dot(weights.astype(jnp.bfloat16), grads, preferred_element_type=jnp.float32)
        return carry

    lax.fori_loop(0, queries.shape[0] // rows, step, 0)
    kv_grad[...] = totals[...].astype(jnp.bfloat16)


VMEM = pl.BlockSpec(memory_space=pltpu.VMEM)
HBM = pl.BlockSpec(memory_space=pl.ANY)


def call(kernel, outs, ins, in_specs, out_specs, scratch, identity=None, copies=0, locals_=0, limit=None):
    if copies:
        scratch = list(scratch) + [
            pltpu.SemaphoreType.DMA((copies,)),
            pltpu.SemaphoreType.DMA((copies,)),
            pltpu.SemaphoreType.DMA((locals_,)),
        ]
    return pl.pallas_call(
        kernel,
        out_shape=outs,
        in_specs=in_specs,
        out_specs=out_specs,
        scratch_shapes=scratch,
        compiler_params=pltpu.CompilerParams(
            collective_id=identity,
            has_side_effects=identity is not None,
            vmem_limit_bytes=limit and limit * 2**20,
        ),
    )(*ins)


def shape(*dims):
    return jax.ShapeDtypeStruct(dims, jnp.bfloat16)


def body(normed, w_qkv, w_out, block_order, d_out):
    rows, model = normed.shape[1], normed.shape[2]
    block_rows = rows // 2
    part = w_out.shape[0]
    length = rows * lax.axis_size("ctx")
    y = lax.axis_index("dp")
    query_pos = stored_positions(
        block_order,
        lax.axis_index("ctx") * rows + jnp.arange(rows, dtype=jnp.int32),
        block_rows,
    )
    all_pos = stored_positions(block_order, jnp.arange(length, dtype=jnp.int32), block_rows)
    cosine, sines = rope_tables(query_pos, HD)

    all_normed, all_d_out, full_q, full_kv, full_out = call(
        front_kernel,
        [
            shape(4, rows, model),
            shape(4, rows, model),
            shape(4, 4, 4, part, HD),
            shape(4, 4, 4, part, HD),
            shape(4, 4, 4, part, HD),
        ],
        [normed[0], d_out[0], w_qkv, w_out],
        [HBM] * 4,
        [HBM] * 5,
        [pltpu.VMEM((2, rows, model), jnp.bfloat16)],
        identity=1,
        copies=3 * 10 + 2 * 8,
        locals_=5,
    )
    full_q, full_kv, full_out = (full.reshape(model, HD) for full in (full_q, full_kv, full_out))

    projected = jnp.dot(
        all_normed.reshape(4 * rows, model),
        jnp.concatenate([full_q, full_kv], axis=1),
        preferred_element_type=jnp.float32,
    ).reshape(4, rows, 2 * HD)
    head_grads = (
        jnp.dot(all_d_out.reshape(4 * rows, model), full_out, preferred_element_type=jnp.float32)
        .astype(jnp.bfloat16)
        .reshape(4, rows, HD)
    )
    queries = projected[:, :, :HD]
    queries = (queries * cosine + swap_halves(queries) * sines).astype(jnp.bfloat16)
    kv = jnp.stack(
        [
            lax.dynamic_index_in_dim(projected, lax.rem(y + k, 4), 0, keepdims=False)[:, HD:]
            for k in (0, 1)
        ]
    )
    turned = kv * cosine + swap_halves(kv) * sines
    kv = jnp.where(lax.rem(y, 2) == 0, turned, kv).astype(jnp.bfloat16)
    all_queries, all_grads, all_kv = call(
        middle_kernel,
        [shape(4, rows, HD), shape(4, rows, HD), shape(2, 4, 4, rows, HD)],
        [queries, head_grads, kv],
        [HBM] * 3,
        [HBM] * 3,
        [],
        identity=2,
        copies=1 + 6 + 3 + 4,
        locals_=3,
    )
    heads_out, query_grad, kv_terms = call(
        attention_kernel,
        [shape(4 * rows, HD), shape(4 * rows, HD), shape(2, length, HD)],
        [
            jnp.concatenate([query_pos, query_pos])[None, :],
            all_pos[:, None],
            jnp.concatenate([cosine, cosine]),
            jnp.concatenate([sines, sines]),
            all_queries.reshape(4 * rows, HD),
            all_grads.reshape(4 * rows, HD),
            all_kv.reshape(2, length, HD),
        ],
        [VMEM] * 7,
        [VMEM] * 3,
        [pltpu.VMEM((2, length, HD), jnp.float32)],
        limit=40,
    )
    width = model // 4
    attn_out, d_normed, d_w_qkv, d_w_out = call(
        back_kernel,
        [shape(rows, width), shape(rows, width), shape(*w_qkv.shape), shape(*w_out.shape)],
        [
            heads_out.reshape(4, rows, HD),
            query_grad.reshape(4, rows, HD),
            kv_terms.reshape(2, 4, 4, rows, HD),
            cosine,
            sines,
            all_normed,
            all_d_out,
            full_q,
            full_kv,
            full_out,
        ],
        [HBM, HBM, VMEM, VMEM, VMEM, HBM, HBM, HBM, HBM, HBM],
        [VMEM] * 4,
        [
            (
                sum_kv_scratch(rows),
                sum_groups_scratch(rows, width),
                sum_groups_scratch(rows, width),
                sum_weight_scratch(part),
                sum_weight_scratch(part),
                sum_weight_scratch(part),
            ),
            (
                pltpu.VMEM((4, rows, model), jnp.bfloat16),
                pltpu.VMEM((4, rows, model), jnp.bfloat16),
                pltpu.VMEM((model, 2 * HD), jnp.bfloat16),
                pltpu.VMEM((model, HD), jnp.bfloat16),
            ),
            pltpu.VMEM((4, rows, HD), jnp.bfloat16),
            pltpu.VMEM((4, rows, 2 * HD), jnp.bfloat16),
        ],
        identity=3,
        copies=10 + 6 + 2 * 9 + 3 * 12,
        locals_=7,
        limit=56,
    )
    return attn_out[None], d_normed[None], d_w_qkv, d_w_out


def solution(mesh):
    in_specs = (
        P("dp", "ctx", None),
        P(("dp", "ctx"), "tp"),
        P(("dp", "ctx"), "tp"),
        P(),
        P("dp", "ctx", None),
    )
    out_specs = (
        P("dp", "ctx", "tp"),
        P("dp", "ctx", "tp"),
        P(("dp", "ctx"), "tp"),
        P(("dp", "ctx"), "tp"),
    )
    return jax.shard_map(body, mesh=mesh, in_specs=in_specs, out_specs=out_specs, check_vma=False)
```

```python
import jax
import jax.numpy as jnp
from jax import lax
from jax.experimental import pallas as pl
from jax.experimental.pallas import tpu as pltpu
from jax.sharding import PartitionSpec as P

HD = 128
SIDE = 4
MESH = pl.DeviceIdType.MESH

rope_base = 500000.0
masked_score = -1e30
contract_last = (((1,), (1,)), ((), ()))
contract_first = (((0,), (0,)), ((), ()))


def stored_positions(order, row_ids, block_rows):
    owner = row_ids // block_rows
    matches = owner[:, None] == jnp.arange(order.shape[0], dtype=jnp.int32)[None, :]
    picked = jnp.sum(jnp.where(matches, order[None, :], 0), axis=1)
    return picked * block_rows + row_ids % block_rows


def rope_tables(positions, head_size):
    half_size = head_size // 2
    frequency = rope_base ** (-2.0 * jnp.arange(half_size, dtype=jnp.float32) / head_size)
    angles = positions.astype(jnp.float32)[:, None] * frequency[None, :]
    sines = jnp.sin(angles)
    cosine = jnp.cos(angles)
    return (
        jnp.concatenate([cosine, cosine], axis=1),
        jnp.concatenate([-sines, sines], axis=1),
    )


class Links:
    def __init__(self, send, recv):
        self.send, self.recv, self.used, self.copies = send, recv, 0, []
        self.y = lax.axis_index("dp")
        self.c = lax.axis_index("ctx")
        self.t = lax.axis_index("tp")
        self.x = self.c // SIDE
        self.z = self.c % SIDE
        self.core = lax.rem(self.t, 2)
        self.side = self.t // 2

    def along_y(self, k):
        return (lax.rem(self.y + k, SIDE), self.c, self.t)

    def along_x(self, k):
        return (self.y, lax.rem(self.x + k, SIDE) * SIDE + self.z, self.t)

    def along_z(self, k):
        return (self.y, self.x * SIDE + lax.rem(self.z + k, SIDE), self.t)

    def other_core(self):
        return (self.y, self.c, self.t + 1 - 2 * self.core)

    def other_side(self):
        return (self.y, self.c, lax.rem(self.t + 2, 4))

    def greet(self):
        partners = (
            [self.along_y(k) for k in (1, 2, 3)]
            + [self.along_z(k) for k in (1, 2, 3)]
            + [self.along_x(1), self.along_x(3), self.other_core(), self.other_side()]
        )
        barrier = pltpu.get_barrier_semaphore()
        for partner in partners:
            pl.semaphore_signal(barrier, inc=1, device_id=partner, device_id_type=MESH)
        pl.semaphore_wait(barrier, len(partners))

    def copy(self, source, target, partner):
        made = pltpu.make_async_remote_copy(
            src_ref=source,
            dst_ref=target,
            send_sem=self.send.at[self.used],
            recv_sem=self.recv.at[self.used],
            device_id=partner,
            device_id_type=MESH,
        )
        made.start()
        self.used += 1
        self.copies.append(made)
        return made

    def finish(self):
        for made in self.copies:
            made.wait_send()


def local_copy(source, target, semaphore):
    made = pltpu.make_async_copy(source, target, semaphore)
    made.start()
    return made


def in_order(streams, order):
    for name in order:
        next(streams[name], None)


def to_end(streams):
    for stream in streams.values():
        for _ in stream:
            pass


def column(i, width=HD):
    return pl.ds(pl.multiple_of(i * width, width), width)


def ring_gather(links, along, here, view, arrived=None):
    before, after, across = (
        lax.rem(here + 3, SIDE),
        lax.rem(here + 1, SIDE),
        lax.rem(here + 2, SIDE),
    )
    arrived = arrived or (lambda block: None)
    own = view(here, None)
    right = links.copy(own, own, along(1))
    left = links.copy(own, own, along(3))
    yield
    right.wait_recv()
    passed = view(before, 0)
    onward = links.copy(passed, passed, along(1))
    left.wait_recv()
    passed = view(after, 1)
    back = links.copy(passed, passed, along(3))
    arrived(view(before, None))
    arrived(view(after, None))
    yield
    onward.wait_recv()
    arrived(view(across, 0))
    back.wait_recv()
    arrived(view(across, 1))


def gather_columns(links, source, chosen, full):
    y, x, z = links.y, links.x, links.z
    place = full.at[y, x, z]
    copies = [
        links.copy(source.at[:, column(chosen(lax.rem(y + k, SIDE)))], place, links.along_y(k))
        for k in (2, 1, 3)
    ]
    yield
    for made in copies:
        made.wait_recv()
    block = full.at[:, x, z]
    copies = [links.copy(block, block, links.along_z(k)) for k in (2, 1, 3)]
    yield
    for made in copies:
        made.wait_recv()
    yield from ring_gather(
        links,
        links.along_x,
        x,
        lambda i, h: full.at[:, i] if h is None else full.at[pl.ds(2 * h, 2), i],
    )


def gather_tokens(links, full):
    half = full.shape[1] // 2
    first = pl.multiple_of(links.core * half, half)
    handed = []

    def view(i, h):
        if h is None:
            return full.at[i, pl.ds(first, half)]
        return full.at[i, pl.ds(pl.multiple_of(first + h * (half // 2), half // 2), half // 2)]

    def hand(block):
        handed.append(links.copy(block, block, links.other_core()))

    yield from ring_gather(links, links.along_y, links.y, view, hand)
    yield
    for made in handed:
        made.wait_recv()


def gather_kind(links, full):
    x, z = links.x, links.z
    block = full.at[x, z]
    copies = [links.copy(block, block, links.along_z(k)) for k in (2, 1, 3)]
    yield
    for made in copies:
        made.wait_recv()
    yield from ring_gather(
        links,
        links.along_x,
        x,
        lambda i, h: full.at[i] if h is None else full.at[i, pl.ds(2 * h, 2)],
    )


def exchange_heads(links, source, place, own_semaphore):
    copies = [
        links.copy(source.at[lax.rem(links.y + k, SIDE)], place, links.along_y(k))
        for k in (2, 1, 3)
    ]
    return copies, local_copy(source.at[links.y], place, own_semaphore)


def add_blocks(target, *terms):
    lead, (height, width) = target.shape[:-2], target.shape[-2:]
    rows = min(height, max(16, 16384 // width))
    per = height // rows
    count = per
    for size in lead:
        count *= size

    def step(i, carry):
        at = (pl.ds(pl.multiple_of(i % per * rows, rows), rows),)
        rest = i // per
        for size in lead[::-1]:
            at = (rest % size,) + at
            rest = rest // size
        total = terms[0][at].astype(jnp.float32)
        for term in terms[1:]:
            total = total + term[at].astype(jnp.float32)
        target[at] = total.astype(target.dtype)
        return carry

    lax.fori_loop(0, count, step, 0)


def ring_sum(links, along, here, view, result, scratch, prepare=None):
    passing, from_left, from_right = scratch
    left, right, across = (
        lax.rem(here + 3, SIDE),
        lax.rem(here + 1, SIDE),
        lax.rem(here + 2, SIDE),
    )
    prepare = prepare or (lambda i: None)
    prepare(across)
    first = links.copy(view(across, 0), passing.at[0], along(1))
    second = links.copy(view(across, 1), passing.at[1], along(3))
    prepare(right)
    plain_right = links.copy(view(right, 1), from_left.at[1], along(1))
    prepare(left)
    plain_left = links.copy(view(left, 0), from_right.at[0], along(3))
    yield
    prepare(here)
    first.wait_recv()
    add_blocks(passing.at[0], passing.at[0], view(right, 0))
    summed_right = links.copy(passing.at[0], from_left.at[0], along(1))
    second.wait_recv()
    add_blocks(passing.at[1], passing.at[1], view(left, 1))
    summed_left = links.copy(passing.at[1], from_right.at[1], along(3))
    yield
    plain_left.wait_recv()
    summed_right.wait_recv()
    add_blocks(result(0), view(here, 0), from_left.at[0], from_right.at[0])
    plain_right.wait_recv()
    summed_left.wait_recv()
    add_blocks(result(1), view(here, 1), from_left.at[1], from_right.at[1])


def sum_weight(links, tokens, grads, scratch):
    terms, ring, middle, arrived, summed, placed = scratch
    y, x, z = links.y, links.x, links.z
    size = 4 * terms.shape[3]

    def prepare(i):
        def step(owner, carry):
            at = column(owner * SIDE + i, size)
            rows = tokens[:, :, at].reshape(-1, size)
            part = lax.dot_general(
                rows,
                grads[...].reshape(rows.shape[0], HD),
                contract_first,
                preferred_element_type=jnp.float32,
            )
            terms[owner, i] = part.astype(jnp.bfloat16).reshape(terms.shape[2:])
            return carry

        lax.fori_loop(0, SIDE, step, 0)

    yield from ring_sum(
        links,
        links.along_x,
        x,
        lambda i, h: terms.at[pl.ds(2 * h, 2), i],
        lambda h: middle.at[pl.ds(2 * h, 2)],
        ring,
        prepare,
    )
    copies = [
        links.copy(middle.at[:, lax.rem(z + k, SIDE)], arrived.at[k - 1], links.along_z(k))
        for k in (2, 1, 3)
    ]
    yield
    for made in copies:
        made.wait_recv()
    add_blocks(summed, middle.at[:, z], arrived.at[0], arrived.at[1], arrived.at[2])
    copies = [
        links.copy(summed.at[lax.rem(y + k, SIDE)], placed.at[y], links.along_y(k))
        for k in (2, 1, 3)
    ]
    placed[y] = summed[y]
    yield
    for made in copies:
        made.wait_recv()


def sum_weight_scratch(rows):
    def vmem(*dims):
        return pltpu.VMEM(dims + (rows, HD), jnp.bfloat16)

    ring = (vmem(2, 2, 4), vmem(2, 2, 4), vmem(2, 2, 4))
    return (vmem(4, 4, 4), ring, vmem(4, 4), vmem(3, 4), vmem(4), vmem(4))


def sum_groups(links, rows, weights, result, start, scratch):
    terms, near, ring, paired, far = scratch
    whole, width = result.shape[1], terms.shape[3]
    core, side = links.core, links.side
    size = 256

    def prepare(owner):
        def step(i, carry):
            at = owner * (whole // size) + start // size + i
            part = lax.dot_general(
                rows[...].reshape(-1, rows.shape[2]),
                model_rows(weights, at, size),
                contract_last,
                preferred_element_type=jnp.float32,
            )
            terms[owner, :, :, column(i, size)] = part.astype(jnp.bfloat16).reshape(
                SIDE, rows.shape[1], size
            )
            return carry

        lax.fori_loop(0, width // size, step, 0)

    handed = []
    for i in range(2):
        prepare(2 * i + 1 - core)
        handed.append(links.copy(terms.at[2 * i + 1 - core], near.at[i], links.other_core()))
    for i in range(2):
        prepare(2 * i + core)
    yield
    for i in range(2):
        handed[i].wait_recv()
        add_blocks(terms.at[2 * i + core], terms.at[2 * i + core], near.at[i])
    yield from ring_sum(
        links,
        links.along_y,
        links.y,
        lambda i, h: terms.at[2 * h + core, i],
        lambda h: paired.at[h],
        ring,
    )
    across = links.copy(paired.at[1 - side], far, links.other_side())
    yield
    across.wait_recv()
    add_blocks(result.at[:, pl.ds(start, width)], paired.at[side], far)


def sum_groups_scratch(rows, width):
    def vmem(*dims):
        return pltpu.VMEM(dims + (rows, width), jnp.bfloat16)

    return (vmem(4, 4), vmem(2, 4), (vmem(2), vmem(2), vmem(2)), vmem(2), vmem())


def model_rows(weights, i, size):
    parts = [weight[i // 4, i % 4].reshape(size, weight.shape[4]) for weight in weights]
    return parts[0] if len(parts) == 1 else jnp.concatenate(parts, axis=1)


def sum_kind(links, terms, scratch):
    ring, middle, arrived, total = scratch
    x, z = links.x, links.z
    yield from ring_sum(
        links,
        links.along_x,
        x,
        lambda i, h: terms.at[i, pl.ds(2 * h, 2)],
        lambda h: middle.at[pl.ds(2 * h, 2)],
        ring,
    )
    copies = [
        links.copy(middle.at[lax.rem(z + k, SIDE)], arrived.at[k - 1], links.along_z(k))
        for k in (2, 1, 3)
    ]
    yield
    for made in copies:
        made.wait_recv()
    add_blocks(total, middle.at[z], arrived.at[0], arrived.at[1], arrived.at[2])


def sum_kind_scratch(rows):
    def vmem(*dims):
        return pltpu.VMEM(dims + (rows, HD), jnp.bfloat16)

    return ((vmem(2, 2), vmem(2, 2), vmem(2, 2)), vmem(4), vmem(3), pltpu.VMEM((rows, HD), jnp.float32))


def hand_kv(links, key_total, value_total, cosine, sines, grads, handed):
    y = links.y
    key, value = key_total[...], value_total[...]
    key = key * cosine[...] - pltpu.roll(key, HD // 2, 1) * sines[...]
    keeps_key = lax.rem(y, 2) == 0
    handed[...] = jnp.where(keeps_key, value, key).astype(jnp.bfloat16)
    passed = links.copy(handed, grads.at[y, :, pl.ds(HD, HD)], links.along_y(3))
    grads[y, :, HD:] = jnp.where(keeps_key, key, value).astype(jnp.bfloat16)
    yield
    passed.wait_recv()


def project(tokens, weight, target):
    size = 1024

    def step(i, carry):
        rows = tokens[:, :, column(i, size)]
        part = jnp.dot(
            rows.reshape(-1, size),
            weight[i].reshape(size, HD),
            preferred_element_type=jnp.float32,
        ).reshape(target.shape)
        target[...] = jnp.where(i == 0, part, target[...] + part)
        return carry

    lax.fori_loop(0, SIDE, step, 0)


def attend(query_pos, key_pos, cosine, sines, queries, head_grads, kv, heads_out, query_grad, totals):
    score_scale = HD ** (-0.5)
    length = key_pos.shape[0]
    pair = 2
    rows = pair * queries.shape[1]
    keys, values = kv[0].reshape(length, HD), kv[1].reshape(length, HD)
    keys_t, values_t = keys.T, values.T
    turn = jnp.concatenate([cosine[...]] * pair), jnp.concatenate([sines[...]] * pair)
    totals[...] = jnp.zeros_like(totals)

    def step(i, carry):
        at = pl.ds(i * pair, pair)
        q, grads = queries[at].reshape(rows, HD), head_grads[at].reshape(rows, HD)
        allowed = key_pos[...] <= query_pos[...]
        scores = (
            lax.dot_general(keys, q, contract_last, preferred_element_type=jnp.float32) * score_scale
        )
        scores = jnp.where(allowed, scores, masked_score)
        row_max = jnp.max(scores, axis=0, keepdims=True)
        raw = jnp.where(allowed, jnp.exp(scores - row_max), 0.0)
        row_sum = jnp.sum(raw, axis=0, keepdims=True)
        weighted = jnp.dot(values_t, raw.astype(jnp.bfloat16), preferred_element_type=jnp.float32)
        out = (weighted / row_sum).astype(jnp.bfloat16).astype(jnp.float32)
        row_dots = jnp.sum(grads.astype(jnp.float32).T * out, axis=0, keepdims=True)
        weights = raw * (1.0 / row_sum)
        dweights = lax.dot_general(values, grads, contract_last, preferred_element_type=jnp.float32)
        dscores = (weights * (dweights - row_dots)).astype(jnp.bfloat16)
        heads_out[at] = out.T.astype(jnp.bfloat16).reshape(pair, -1, HD)
        dq = jnp.dot(keys_t, dscores, preferred_element_type=jnp.float32).T * score_scale
        dq = dq * turn[0] - pltpu.roll(dq, HD // 2, 1) * turn[1]
        query_grad[at] = dq.astype(jnp.bfloat16).reshape(pair, -1, HD)
        totals[0] += jnp.dot(dscores, q, preferred_element_type=jnp.float32) * score_scale
        totals[1] += jnp.dot(weights.astype(jnp.bfloat16), grads, preferred_element_type=jnp.float32)
        return carry

    lax.fori_loop(0, queries.shape[0] // pair, step, 0)


def whole_kernel(
    normed, d_out, w_qkv, w_out, query_pos, key_pos, cosine, sines,
    attn_out, d_normed, d_w_qkv, d_w_out,
    tokens, weights, blocks, wide, rows_kv, sums, send, recv, local,
):
    links = Links(send, recv)
    y, x, z = links.y, links.x, links.z
    heads = w_out.shape[1] // HD
    all_normed, all_d_out = tokens
    full_q, full_kv, full_out = weights
    my_queries, my_grads, queries, head_grads, heads_out, query_grad, all_heads = blocks
    projected, grads = wide
    my_kv, all_kv, totals, kv_terms, handed = rows_kv
    after = lax.rem(y + 1, SIDE)

    given = {
        "q": (w_qkv, lambda j: j, full_q),
        "k": (w_qkv, lambda j: heads + lax.rem(j, 2), full_kv),
        "o": (w_out, lambda j: j, full_out),
    }
    mine = [
        local_copy(source.at[:, column(chosen(y))], full.at[y, x, z], local.at[i])
        for i, (source, chosen, full) in enumerate(given.values())
    ]
    mine += [
        local_copy(source.at[0], full.at[y], local.at[3 + i])
        for i, (source, full) in enumerate(((normed, all_normed), (d_out, all_d_out)))
    ]
    for k in (2, 3):
        grads[lax.rem(y + k, SIDE), :, HD:] = jnp.zeros_like(grads[0, :, HD:])
    links.greet()
    streams = {name: gather_columns(links, *parts) for name, parts in given.items()}
    streams["n"] = gather_tokens(links, all_normed)
    streams["d"] = gather_tokens(links, all_d_out)
    for made in mine:
        made.wait()
    in_order(streams, "qknoqkoqndkqkoqnknnqk")

    project(all_normed.at[pl.ds(0, SIDE)], full_kv, projected)
    for i, sequence in enumerate((y, after)):
        part = projected[sequence]
        turned = part * cosine[...] + pltpu.roll(part, HD // 2, 1) * sines[...]
        my_kv[i] = jnp.where(lax.rem(y, 2) == 0, turned, part).astype(jnp.bfloat16)
    place = all_kv.at[lax.rem(y, 2), x, z]
    passed = links.copy(my_kv.at[1], place, links.along_y(1))
    place[...] = my_kv[0]
    project(all_normed, full_q, projected)
    for i in range(SIDE):
        part = projected[i]
        turned = part * cosine[...] + pltpu.roll(part, HD // 2, 1) * sines[...]
        my_queries[i] = turned.astype(jnp.bfloat16)
    passed.wait_recv()
    streams["K"] = gather_kind(links, all_kv.at[0])
    streams["V"] = gather_kind(links, all_kv.at[1])
    in_order(streams, "KV")
    query_copies, query_mine = exchange_heads(links, my_queries, queries.at[y], local.at[0])
    in_order(streams, "odKVoddooddd")
    project(all_d_out, full_out, projected)
    my_grads[...] = projected[...].astype(jnp.bfloat16)
    grad_copies, grad_mine = exchange_heads(links, my_grads, head_grads.at[y], local.at[1])
    in_order(streams, "KVKV")
    to_end(streams)
    for made in query_copies + grad_copies:
        made.wait_recv()
    query_mine.wait()
    grad_mine.wait()

    attend(query_pos, key_pos, cosine, sines, queries, head_grads, all_kv, heads_out, query_grad, totals)
    kv_terms[...] = totals[...].astype(jnp.bfloat16).reshape(kv_terms.shape)

    streams = {
        "K": sum_kind(links, kv_terms.at[0], sums[0]),
        "V": sum_kind(links, kv_terms.at[1], sums[1]),
    }
    in_order(streams, "KV")
    head_copies, head_mine = exchange_heads(links, heads_out, all_heads.at[y], local.at[0])
    grad_copies, grad_mine = exchange_heads(
        links, query_grad, grads.at[y, :, pl.ds(0, HD)], local.at[1]
    )
    for made in head_copies:
        made.wait_recv()
    head_mine.wait()
    half = sums[2][0].shape[3]
    qkv = (full_q, full_kv)
    streams["a"] = sum_groups(links, all_heads, (full_out,), attn_out, 0, sums[2])
    streams["b"] = sum_groups(links, all_heads, (full_out,), attn_out, half, sums[3])
    streams["o"] = sum_weight(links, all_d_out, all_heads, sums[6])
    streams["q"] = sum_weight(links, all_normed, grads.at[:, :, pl.ds(0, HD)], sums[7])
    in_order(streams, "aKVbaKoVK")
    for made in grad_copies:
        made.wait_recv()
    grad_mine.wait()
    in_order(streams, "qV")
    streams["h"] = hand_kv(links, sums[0][3], sums[1][3], cosine, sines, grads, handed)
    in_order(streams, "hbaoh")
    streams["n"] = sum_groups(links, grads, qkv, d_normed, 0, sums[4])
    streams["m"] = sum_groups(links, grads, qkv, d_normed, half, sums[5])
    streams["w"] = sum_weight(links, all_normed, grads.at[:, :, pl.ds(HD, HD)], sums[8])
    in_order(streams, "nqmbnwmaoqbwnmaoqwbnmoqwnmw")
    to_end(streams)
    links.finish()
    placed_out, placed_q, placed_kv = sums[6][5], sums[7][5], sums[8][5]
    width = SIDE * HD
    for j in range(SIDE):
        d_w_out[:, j * HD : (j + 1) * HD] = placed_out[j]
        d_w_qkv[:, j * HD : (j + 1) * HD] = placed_q[j]
    for kind in range(2):
        total = placed_kv[kind].astype(jnp.float32) + placed_kv[kind + 2].astype(jnp.float32)
        d_w_qkv[:, width + kind * HD : width + (kind + 1) * HD] = total.astype(jnp.bfloat16)


def hand_on_kernel(*refs):
    half = len(refs) // 2
    for source, target in zip(refs[:half], refs[half:]):
        target[...] = source[...].reshape(target.shape)


VMEM = pl.BlockSpec(memory_space=pltpu.VMEM)
HBM = pl.BlockSpec(memory_space=pl.ANY)


def shape(*dims):
    return jax.ShapeDtypeStruct(dims, jnp.bfloat16)


def body(normed, w_qkv, w_out, block_order, d_out):
    rows, model = normed.shape[1], normed.shape[2]
    block_rows = rows // 2
    part = w_out.shape[0]
    length = rows * lax.axis_size("ctx")
    query_pos = stored_positions(
        block_order,
        lax.axis_index("ctx") * rows + jnp.arange(rows, dtype=jnp.int32),
        block_rows,
    )
    all_pos = stored_positions(block_order, jnp.arange(length, dtype=jnp.int32), block_rows)
    cosine, sines = rope_tables(query_pos, HD)
    width = model // 4

    def vmem(*dims, kind=jnp.bfloat16):
        return pltpu.VMEM(dims, kind)

    blocks = vmem(4, rows, HD)
    copies = 5 * 8 + 2 * 3 + 1 + 2 * 7 + 4 * 3 + 2 * 9 + 1 + 4 * 9 + 3 * 12
    outs = [shape(rows, width), shape(rows, width), shape(*w_qkv.shape), shape(*w_out.shape)]
    results = pl.pallas_call(
        whole_kernel,
        out_shape=outs,
        in_specs=[HBM] * 4 + [VMEM] * 4,
        out_specs=[VMEM] * 4,
        scratch_shapes=[
            (vmem(4, rows, model),) * 2,
            (vmem(4, 4, 4, part, HD),) * 3,
            (blocks,) * 7,
            (vmem(4, rows, HD, kind=jnp.float32), vmem(4, rows, 2 * HD)),
            (
                vmem(2, rows, HD),
                vmem(2, 4, 4, rows, HD),
                vmem(2, length, HD, kind=jnp.float32),
                vmem(2, 4, 4, rows, HD),
                vmem(rows, HD),
            ),
            (sum_kind_scratch(rows),) * 2
            + (sum_groups_scratch(rows, width // 2),) * 4
            + (sum_weight_scratch(part),) * 3,
            pltpu.SemaphoreType.DMA((copies,)),
            pltpu.SemaphoreType.DMA((copies,)),
            pltpu.SemaphoreType.DMA((5,)),
        ],
        compiler_params=pltpu.CompilerParams(
            collective_id=1, has_side_effects=True, vmem_limit_bytes=60 * 2**20
        ),
    )(
        normed,
        d_out,
        w_qkv,
        w_out,
        jnp.concatenate([query_pos, query_pos])[None, :],
        all_pos[:, None],
        cosine,
        sines,
    )
    outs = [shape(1, rows, width)] * 2 + outs[2:]
    return pl.pallas_call(hand_on_kernel, out_shape=outs)(*results)


def solution(mesh):
    in_specs = (
        P("dp", "ctx", None),
        P(("dp", "ctx"), "tp"),
        P(("dp", "ctx"), "tp"),
        P(),
        P("dp", "ctx", None),
    )
    out_specs = (
        P("dp", "ctx", "tp"),
        P("dp", "ctx", "tp"),
        P(("dp", "ctx"), "tp"),
        P(("dp", "ctx"), "tp"),
    )
    return jax.shard_map(body, mesh=mesh, in_specs=in_specs, out_specs=out_specs, check_vma=False)
```

```python
import jax
import jax.numpy as jnp
import numpy as np
from jax import lax
from jax.experimental import pallas as pl
from jax.experimental.pallas import tpu as pltpu
from jax.sharding import PartitionSpec as P

HD = 128
SIDE = 4
MESH = pl.DeviceIdType.MESH

rope_base = 500000.0
masked_score = -1e30
contract_last = (((1,), (1,)), ((), ()))
contract_first = (((0,), (0,)), ((), ()))


class Links:
    def __init__(self, send, recv):
        self.send, self.recv, self.used, self.copies = send, recv, 0, []
        self.y = lax.axis_index("dp")
        self.c = lax.axis_index("ctx")
        self.t = lax.axis_index("tp")
        self.x = self.c // SIDE
        self.z = self.c % SIDE
        self.core = lax.rem(self.t, 2)
        self.side = self.t // 2

    def along_y(self, k):
        return (lax.rem(self.y + k, SIDE), self.c, self.t)

    def along_x(self, k):
        return (self.y, lax.rem(self.x + k, SIDE) * SIDE + self.z, self.t)

    def along_z(self, k):
        return (self.y, self.x * SIDE + lax.rem(self.z + k, SIDE), self.t)

    def other_core(self):
        return (self.y, self.c, self.t + 1 - 2 * self.core)

    def other_side(self):
        return (self.y, self.c, lax.rem(self.t + 2, 4))

    def greet(self):
        partners = (
            [self.along_y(k) for k in (1, 2, 3)]
            + [self.along_z(k) for k in (1, 2, 3)]
            + [self.along_x(1), self.along_x(3), self.other_core(), self.other_side()]
        )
        barrier = pltpu.get_barrier_semaphore()
        for partner in partners:
            pl.semaphore_signal(barrier, inc=1, device_id=partner, device_id_type=MESH)
        pl.semaphore_wait(barrier, len(partners))

    def copy(self, source, target, partner):
        made = pltpu.make_async_remote_copy(
            src_ref=source,
            dst_ref=target,
            send_sem=self.send.at[self.used],
            recv_sem=self.recv.at[self.used],
            device_id=partner,
            device_id_type=MESH,
        )
        made.start()
        self.used += 1
        self.copies.append(made)
        return made

    def finish(self):
        for made in self.copies:
            made.wait_send()


def local_copy(source, target, semaphore):
    made = pltpu.make_async_copy(source, target, semaphore)
    made.start()
    return made


def in_order(streams, order):
    for name in order:
        next(streams[name], None)


def to_end(streams):
    for stream in streams.values():
        for _ in stream:
            pass


def column(i, width=HD):
    return pl.ds(pl.multiple_of(i * width, width), width)


def ring_gather(links, along, here, view, arrived=None):
    before, after, across = (
        lax.rem(here + 3, SIDE),
        lax.rem(here + 1, SIDE),
        lax.rem(here + 2, SIDE),
    )
    arrived = arrived or (lambda block: None)
    own = view(here, None)
    right = links.copy(own, own, along(1))
    left = links.copy(own, own, along(3))
    yield
    right.wait_recv()
    passed = view(before, 0)
    onward = links.copy(passed, passed, along(1))
    left.wait_recv()
    passed = view(after, 1)
    back = links.copy(passed, passed, along(3))
    arrived(view(before, None))
    arrived(view(after, None))
    yield
    onward.wait_recv()
    arrived(view(across, 0))
    back.wait_recv()
    arrived(view(across, 1))


def gather_columns(links, source, chosen, full):
    y, x, z = links.y, links.x, links.z
    place = full.at[y, x, z]
    copies = [
        links.copy(source.at[:, column(chosen(lax.rem(y + k, SIDE)))], place, links.along_y(k))
        for k in (2, 1, 3)
    ]
    yield
    for made in copies:
        made.wait_recv()
    block = full.at[:, x, z]
    copies = [links.copy(block, block, links.along_z(k)) for k in (2, 1, 3)]
    yield
    for made in copies:
        made.wait_recv()
    yield from ring_gather(
        links,
        links.along_x,
        x,
        lambda i, h: full.at[:, i] if h is None else full.at[pl.ds(2 * h, 2), i],
    )


def gather_tokens(links, full):
    half = full.shape[1] // 2
    first = pl.multiple_of(links.core * half, half)
    handed = []

    def view(i, h):
        if h is None:
            return full.at[i, pl.ds(first, half)]
        return full.at[i, pl.ds(pl.multiple_of(first + h * (half // 2), half // 2), half // 2)]

    def hand(block):
        handed.append(links.copy(block, block, links.other_core()))

    yield from ring_gather(links, links.along_y, links.y, view, hand)
    yield
    for made in handed:
        made.wait_recv()


def gather_kind(links, full):
    x, z = links.x, links.z
    block = full.at[x, z]
    copies = [links.copy(block, block, links.along_z(k)) for k in (2, 1, 3)]
    yield
    for made in copies:
        made.wait_recv()
    yield from ring_gather(
        links,
        links.along_x,
        x,
        lambda i, h: full.at[i] if h is None else full.at[i, pl.ds(2 * h, 2)],
    )


def exchange_heads(links, source, place, own_semaphore):
    copies = [
        links.copy(source.at[lax.rem(links.y + k, SIDE)], place, links.along_y(k))
        for k in (2, 1, 3)
    ]
    return copies, local_copy(source.at[links.y], place, own_semaphore)


def add_blocks(target, *terms):
    lead, (height, width) = target.shape[:-2], target.shape[-2:]
    rows = min(height, max(16, 16384 // width))
    per = height // rows
    count = per
    for size in lead:
        count *= size

    def step(i, carry):
        at = (pl.ds(pl.multiple_of(i % per * rows, rows), rows),)
        rest = i // per
        for size in lead[::-1]:
            at = (rest % size,) + at
            rest = rest // size
        total = terms[0][at].astype(jnp.float32)
        for term in terms[1:]:
            total = total + term[at].astype(jnp.float32)
        target[at] = total.astype(target.dtype)
        return carry

    lax.fori_loop(0, count, step, 0)


def ring_sum(links, along, here, view, result, scratch, prepare=None, extra=None):
    passing, from_left, from_right = scratch
    left, right, across = (
        lax.rem(here + 3, SIDE),
        lax.rem(here + 1, SIDE),
        lax.rem(here + 2, SIDE),
    )
    prepare = prepare or (lambda i: None)
    extra = extra or (lambda h: ())
    prepare(across)
    first = links.copy(view(across, 0), passing.at[0], along(1))
    second = links.copy(view(across, 1), passing.at[1], along(3))
    prepare(right)
    plain_right = links.copy(view(right, 1), from_left.at[1], along(1))
    prepare(left)
    plain_left = links.copy(view(left, 0), from_right.at[0], along(3))
    yield
    prepare(here)
    first.wait_recv()
    add_blocks(passing.at[0], passing.at[0], view(right, 0))
    summed_right = links.copy(passing.at[0], from_left.at[0], along(1))
    second.wait_recv()
    add_blocks(passing.at[1], passing.at[1], view(left, 1))
    summed_left = links.copy(passing.at[1], from_right.at[1], along(3))
    yield
    plain_left.wait_recv()
    summed_right.wait_recv()
    add_blocks(result(0), view(here, 0), from_left.at[0], from_right.at[0], *extra(0))
    plain_right.wait_recv()
    summed_left.wait_recv()
    add_blocks(result(1), view(here, 1), from_left.at[1], from_right.at[1], *extra(1))


def sum_weight(links, tokens, grads, scratch):
    terms, ring, middle, arrived, summed, placed = scratch
    y, x, z = links.y, links.x, links.z
    size = 4 * terms.shape[3]

    def prepare(i):
        def step(owner, carry):
            at = column(owner * SIDE + i, size)
            rows = tokens[:, :, at].reshape(-1, size)
            part = lax.dot_general(
                rows,
                grads[...].reshape(rows.shape[0], HD),
                contract_first,
                preferred_element_type=jnp.float32,
            )
            terms[owner, i] = part.astype(jnp.bfloat16).reshape(terms.shape[2:])
            return carry

        lax.fori_loop(0, SIDE, step, 0)

    yield from ring_sum(
        links,
        links.along_x,
        x,
        lambda i, h: terms.at[pl.ds(2 * h, 2), i],
        lambda h: middle.at[pl.ds(2 * h, 2)],
        ring,
        prepare,
    )
    copies = [
        links.copy(middle.at[:, lax.rem(z + k, SIDE)], arrived.at[k - 1], links.along_z(k))
        for k in (2, 1, 3)
    ]
    yield
    for made in copies:
        made.wait_recv()
    add_blocks(summed, middle.at[:, z], arrived.at[0], arrived.at[1], arrived.at[2])
    copies = [
        links.copy(summed.at[lax.rem(y + k, SIDE)], placed.at[y], links.along_y(k))
        for k in (2, 1, 3)
    ]
    placed[y] = summed[y]
    yield
    for made in copies:
        made.wait_recv()


def sum_weight_scratch(rows):
    def vmem(*dims):
        return pltpu.VMEM(dims + (rows, HD), jnp.bfloat16)

    ring = (vmem(2, 2, 4), vmem(2, 2, 4), vmem(2, 2, 4))
    return (vmem(4, 4, 4), ring, vmem(4, 4), vmem(3, 4), vmem(4), vmem(4))


def sum_groups(links, rows, weight, result, start, scratch, own_part=None):
    terms, near, ring, paired, far = scratch
    whole, width = result.shape[1], terms.shape[3]
    core, side = links.core, links.side
    size = 256

    def prepare(owner):
        def step(i, carry):
            at = owner * (whole // size) + start // size + i
            part = lax.dot_general(
                rows[...].reshape(-1, HD),
                model_rows(weight, at, size),
                contract_last,
                preferred_element_type=jnp.float32,
            )
            terms[owner, :, :, column(i, size)] = part.astype(jnp.bfloat16).reshape(
                SIDE, rows.shape[1], size
            )
            return carry

        lax.fori_loop(0, width // size, step, 0)

    handed = []
    for i in range(2):
        prepare(2 * i + 1 - core)
        handed.append(links.copy(terms.at[2 * i + 1 - core], near.at[i], links.other_core()))
    for i in range(2):
        prepare(2 * i + core)
    yield
    for i in range(2):
        handed[i].wait_recv()
        add_blocks(terms.at[2 * i + core], terms.at[2 * i + core], near.at[i])
    yield from ring_sum(
        links,
        links.along_y,
        links.y,
        lambda i, h: terms.at[2 * h + core, i],
        lambda h: paired.at[h],
        ring,
        extra=None
        if own_part is None
        else lambda h: (own_part.at[2 * h + core, :, pl.ds(start, width)],),
    )
    across = links.copy(paired.at[1 - side], far, links.other_side())
    yield
    across.wait_recv()
    add_blocks(result.at[:, pl.ds(start, width)], paired.at[side], far)


def sum_groups_scratch(rows, width):
    def vmem(*dims):
        return pltpu.VMEM(dims + (rows, width), jnp.bfloat16)

    return (vmem(4, 4), vmem(2, 4), (vmem(2), vmem(2), vmem(2)), vmem(2), vmem())


def model_rows(weight, i, size):
    return weight[i // 4, i % 4].reshape(size, HD)


def own_groups(links, pieces, terms, near):
    core = links.core
    width, size = terms.shape[2], 256

    def prepare(owner):
        def step(i, carry):
            at = owner * (width // size) + i
            part = sum(
                lax.dot_general(
                    rows[...],
                    model_rows(weight, at, size),
                    contract_last,
                    preferred_element_type=jnp.float32,
                )
                for rows, weight in pieces
            )
            terms[owner, :, column(i, size)] = part.astype(jnp.bfloat16)
            return carry

        lax.fori_loop(0, width // size, step, 0)

    handed = []
    for i in range(2):
        prepare(2 * i + 1 - core)
        handed.append(links.copy(terms.at[2 * i + 1 - core], near.at[i], links.other_core()))
    for i in range(2):
        prepare(2 * i + core)
    yield
    for i in range(2):
        handed[i].wait_recv()
        add_blocks(terms.at[2 * i + core], terms.at[2 * i + core], near.at[i])


def sum_kind(links, terms, scratch):
    ring, middle, arrived, total = scratch
    x, z = links.x, links.z
    yield from ring_sum(
        links,
        links.along_x,
        x,
        lambda i, h: terms.at[i, pl.ds(2 * h, 2)],
        lambda h: middle.at[pl.ds(2 * h, 2)],
        ring,
    )
    copies = [
        links.copy(middle.at[lax.rem(z + k, SIDE)], arrived.at[k - 1], links.along_z(k))
        for k in (2, 1, 3)
    ]
    yield
    for made in copies:
        made.wait_recv()
    add_blocks(total, middle.at[z], arrived.at[0], arrived.at[1], arrived.at[2])


def sum_kind_scratch(rows):
    def vmem(*dims):
        return pltpu.VMEM(dims + (rows, HD), jnp.bfloat16)

    return ((vmem(2, 2), vmem(2, 2), vmem(2, 2)), vmem(4), vmem(3), pltpu.VMEM((rows, HD), jnp.float32))


def arrive(exchange):
    copies, own = exchange
    for made in copies:
        made.wait_recv()
    own.wait()


def hand_kv(links, key_total, value_total, cosine, sines, grads, handed):
    y = links.y
    key, value = key_total[...], value_total[...]
    key = key * cosine[...] - pltpu.roll(key, HD // 2, 1) * sines[...]
    keeps_key = lax.rem(y, 2) == 0
    handed[...] = jnp.where(keeps_key, value, key).astype(jnp.bfloat16)
    passed = links.copy(handed, grads.at[y, :, pl.ds(HD, HD)], links.along_y(3))
    grads[y, :, HD:] = jnp.where(keeps_key, key, value).astype(jnp.bfloat16)
    yield
    passed.wait_recv()


def project(tokens, weight, target):
    size = 1024

    def step(i, carry):
        rows = tokens[:, :, column(i, size)]
        part = jnp.dot(
            rows.reshape(-1, size),
            weight[i].reshape(size, HD),
            preferred_element_type=jnp.float32,
        ).reshape(target.shape)
        target[...] = jnp.where(i == 0, part, target[...] + part)
        return carry

    lax.fori_loop(0, SIDE, step, 0)


def attend(query_pos, key_pos, cosine, sines, queries, head_grads, kv, heads_out, query_grad, totals):
    score_scale = HD ** (-0.5)
    length = key_pos.shape[0]
    pair = 2
    rows = pair * queries.shape[1]
    keys, values = kv[0].reshape(length, HD), kv[1].reshape(length, HD)
    keys_t, values_t = keys.T, values.T
    turn = jnp.concatenate([cosine[...]] * pair), jnp.concatenate([sines[...]] * pair)
    totals[...] = jnp.zeros_like(totals)

    def step(i, carry):
        at = pl.ds(i * pair, pair)
        q, grads = queries[at].reshape(rows, HD), head_grads[at].reshape(rows, HD)
        allowed = key_pos[...] <= query_pos[...]
        scores = (
            lax.dot_general(keys, q, contract_last, preferred_element_type=jnp.float32) * score_scale
        )
        scores = jnp.where(allowed, scores, masked_score)
        row_max = jnp.max(scores, axis=0, keepdims=True)
        raw = jnp.where(allowed, jnp.exp(scores - row_max), 0.0)
        row_sum = jnp.sum(raw, axis=0, keepdims=True)
        weighted = jnp.dot(values_t, raw.astype(jnp.bfloat16), preferred_element_type=jnp.float32)
        out = (weighted / row_sum).astype(jnp.bfloat16).astype(jnp.float32)
        row_dots = jnp.sum(grads.astype(jnp.float32).T * out, axis=0, keepdims=True)
        weights = raw * (1.0 / row_sum)
        dweights = lax.dot_general(values, grads, contract_last, preferred_element_type=jnp.float32)
        dscores = (weights * (dweights - row_dots)).astype(jnp.bfloat16)
        heads_out[at] = out.T.astype(jnp.bfloat16).reshape(pair, -1, HD)
        dq = jnp.dot(keys_t, dscores, preferred_element_type=jnp.float32).T * score_scale
        dq = dq * turn[0] - pltpu.roll(dq, HD // 2, 1) * turn[1]
        query_grad[at] = dq.astype(jnp.bfloat16).reshape(pair, -1, HD)
        totals[0] += jnp.dot(dscores, q, preferred_element_type=jnp.float32) * score_scale
        totals[1] += jnp.dot(weights.astype(jnp.bfloat16), grads, preferred_element_type=jnp.float32)
        return carry

    lax.fori_loop(0, queries.shape[0] // pair, step, 0)


def place_tables(links, order, frequency, query_pos, key_pos, cosine, sines):
    rows = cosine.shape[0]
    block = rows // 2
    first, second = order[2 * links.c] * block, order[2 * links.c + 1] * block

    def positions(dims, axis):
        row = lax.rem(lax.broadcasted_iota(jnp.int32, dims, axis), rows)
        return jnp.where(row < block, first, second - block) + row

    query_pos[...] = positions(query_pos.shape, 1)
    angles = positions(cosine.shape, 0).astype(jnp.float32) * frequency[...]
    lane = lax.broadcasted_iota(jnp.int32, sines.shape, 1)
    sine = jnp.sin(angles)
    cosine[...] = jnp.cos(angles)
    sines[...] = jnp.where(lane < HD // 2, -sine, sine)
    row = lax.broadcasted_iota(jnp.int32, (block, 1), 0)
    for i in range(key_pos.shape[0] // block):
        key_pos[i * block : (i + 1) * block] = order[i] * block + row


FRONT = "kqnokvqknoqdvkqnknoPdPVqKoQVdKVdoGKVvKV"
BACK = "KVvbKVbaoKbmVoabKqVahonqmahwbqvewmnemqwnonowamnqw"


def whole_kernel(
    normed, d_out, w_qkv, w_out, order, frequency,
    attn_out, d_normed, d_w_qkv, d_w_out,
    tables, tokens, weights, blocks, wide, rows_kv, own, sums, send, recv, local,
):
    links = Links(send, recv)
    y, x, z = links.y, links.x, links.z
    heads = w_out.shape[1] // HD
    query_pos, key_pos, cosine, sines = tables
    all_normed, all_d_out = tokens
    full_q, full_kv, full_out, full_other = weights
    my_queries, my_grads, queries, head_grads, heads_out, query_grad, all_heads = blocks
    projected, grads = wide
    my_kv, all_kv, totals, kv_terms, handed = rows_kv
    after = lax.rem(y + 1, SIDE)

    given = {
        "k": (w_qkv, lambda j: heads + lax.rem(j, 2), full_kv),
        "q": (w_qkv, lambda j: j, full_q),
        "o": (w_out, lambda j: j, full_out),
        "v": (w_qkv, lambda j: heads + lax.rem(j + 1, 2), full_other),
    }
    mine = [
        local_copy(source.at[:, column(chosen(y))], full.at[y, x, z], local.at[i])
        for i, (source, chosen, full) in enumerate(given.values())
    ]
    mine += [
        local_copy(source.at[0], full.at[y], local.at[4 + i])
        for i, (source, full) in enumerate(((normed, all_normed), (d_out, all_d_out)))
    ]
    for k in (2, 3):
        grads[lax.rem(y + k, SIDE), :, HD:] = jnp.zeros_like(grads[0, :, HD:])
    links.greet()
    streams = {name: gather_columns(links, *parts) for name, parts in given.items()}
    streams["n"] = gather_tokens(links, all_normed)
    streams["d"] = gather_tokens(links, all_d_out)
    for made in mine:
        made.wait()
    in_order(streams, FRONT[:5])
    place_tables(links, order, frequency, query_pos, key_pos, cosine, sines)
    held = {}

    def project_kv():
        for i, sequence in enumerate((y, after)):
            project(all_normed.at[pl.ds(sequence, 1)], full_kv, projected.at[pl.ds(0, 1)])
            part = projected[0]
            turned = part * cosine[...] + pltpu.roll(part, HD // 2, 1) * sines[...]
            my_kv[i] = jnp.where(lax.rem(y, 2) == 0, turned, part).astype(jnp.bfloat16)
        place = all_kv.at[lax.rem(y, 2), x, z]
        passed = links.copy(my_kv.at[1], place, links.along_y(1))
        place[...] = my_kv[0]
        yield
        passed.wait_recv()

    def project_queries():
        project(all_normed, full_q, projected)
        for i in range(SIDE):
            part = projected[i]
            turned = part * cosine[...] + pltpu.roll(part, HD // 2, 1) * sines[...]
            my_queries[i] = turned.astype(jnp.bfloat16)
        held["Q"] = exchange_heads(links, my_queries, queries.at[y], local.at[0])
        yield

    def project_grads():
        project(all_d_out, full_out, projected)
        my_grads[...] = projected[...].astype(jnp.bfloat16)
        held["G"] = exchange_heads(links, my_grads, head_grads.at[y], local.at[1])
        yield

    streams["P"] = project_kv()
    streams["Q"] = project_queries()
    streams["G"] = project_grads()
    streams["K"] = gather_kind(links, all_kv.at[0])
    streams["V"] = gather_kind(links, all_kv.at[1])
    in_order(streams, FRONT[5:])
    arrive(held.pop("Q"))
    arrive(held.pop("G"))
    attend(query_pos, key_pos, cosine, sines, queries, head_grads, all_kv, heads_out, query_grad, totals)
    kv_terms[...] = totals[...].astype(jnp.bfloat16).reshape(kv_terms.shape)

    held["heads"] = exchange_heads(links, heads_out, all_heads.at[y], local.at[0])
    held["grads"] = exchange_heads(links, query_grad, grads.at[y, :, pl.ds(0, HD)], local.at[1])

    def having(name, stream):
        if name in held:
            arrive(held.pop(name))
        yield from stream

    half = sums[2][0].shape[3]
    own_terms, own_near = own
    query_part, kv_part = grads.at[:, :, pl.ds(0, HD)], grads.at[:, :, pl.ds(HD, HD)]
    own_pieces = [(grads.at[y, :, pl.ds(HD, HD)], full_kv), (handed, full_other)]
    streams = {
        "v": streams["v"],
        "K": sum_kind(links, kv_terms.at[0], sums[0]),
        "V": sum_kind(links, kv_terms.at[1], sums[1]),
        "h": hand_kv(links, sums[0][3], sums[1][3], cosine, sines, grads, handed),
        "e": own_groups(links, own_pieces, own_terms, own_near),
        "w": sum_weight(links, all_normed, kv_part, sums[8]),
    }
    for name, needs, stream in (
        ("a", "heads", sum_groups(links, all_heads, full_out, attn_out, 0, sums[2])),
        ("b", "heads", sum_groups(links, all_heads, full_out, attn_out, half, sums[3])),
        ("n", "grads", sum_groups(links, query_part, full_q, d_normed, 0, sums[4], own_terms)),
        ("m", "grads", sum_groups(links, query_part, full_q, d_normed, half, sums[5], own_terms)),
        ("o", "heads", sum_weight(links, all_d_out, all_heads, sums[6])),
        ("q", "grads", sum_weight(links, all_normed, query_part, sums[7])),
    ):
        streams[name] = having(needs, stream)
    in_order(streams, BACK)
    to_end(streams)
    links.finish()
    placed_out, placed_q, placed_kv = sums[6][5], sums[7][5], sums[8][5]
    width = SIDE * HD
    for j in range(SIDE):
        d_w_out[:, j * HD : (j + 1) * HD] = placed_out[j]
        d_w_qkv[:, j * HD : (j + 1) * HD] = placed_q[j]
    for kind in range(2):
        total = placed_kv[kind].astype(jnp.float32) + placed_kv[kind + 2].astype(jnp.float32)
        d_w_qkv[:, width + kind * HD : width + (kind + 1) * HD] = total.astype(jnp.bfloat16)


def hand_on_kernel(*refs):
    half = len(refs) // 2
    for source, target in zip(refs[:half], refs[half:]):
        target[...] = source[...].reshape(target.shape)


VMEM = pl.BlockSpec(memory_space=pltpu.VMEM)
HBM = pl.BlockSpec(memory_space=pl.ANY)


def shape(*dims):
    return jax.ShapeDtypeStruct(dims, jnp.bfloat16)


def body(normed, w_qkv, w_out, block_order, d_out):
    rows, model = normed.shape[1], normed.shape[2]
    part = w_out.shape[0]
    length = rows * lax.axis_size("ctx")
    frequency = rope_base ** (-2.0 * np.arange(HD // 2, dtype=np.float64) / HD)
    frequency = np.tile(frequency, 2).astype(np.float32)[None, :]
    width = model // 4

    def vmem(*dims, kind=jnp.bfloat16):
        return pltpu.VMEM(dims, kind)

    blocks = vmem(4, rows, HD)
    copies = 4 * 10 + 2 * 8 + 1 + 2 * 7 + 4 * 3 + 2 * 9 + 1 + 2 + 4 * 9 + 3 * 12
    outs = [shape(rows, width), shape(rows, width), shape(*w_qkv.shape), shape(*w_out.shape)]
    results = pl.pallas_call(
        whole_kernel,
        out_shape=outs,
        in_specs=[HBM] * 4 + [pl.BlockSpec(memory_space=pltpu.SMEM), VMEM],
        out_specs=[VMEM] * 4,
        scratch_shapes=[
            (
                vmem(1, 2 * rows, kind=jnp.int32),
                vmem(length, 1, kind=jnp.int32),
                vmem(rows, HD, kind=jnp.float32),
                vmem(rows, HD, kind=jnp.float32),
            ),
            (vmem(4, rows, model),) * 2,
            (vmem(4, 4, 4, part, HD),) * 4,
            (blocks,) * 7,
            (vmem(4, rows, HD, kind=jnp.float32), vmem(4, rows, 2 * HD)),
            (
                vmem(2, rows, HD),
                vmem(2, 4, 4, rows, HD),
                vmem(2, length, HD, kind=jnp.float32),
                vmem(2, 4, 4, rows, HD),
                vmem(rows, HD),
            ),
            (vmem(4, rows, width), vmem(2, rows, width)),
            (sum_kind_scratch(rows),) * 2
            + (sum_groups_scratch(rows, width // 2),) * 4
            + (sum_weight_scratch(part),) * 3,
            pltpu.SemaphoreType.DMA((copies,)),
            pltpu.SemaphoreType.DMA((copies,)),
            pltpu.SemaphoreType.DMA((6,)),
        ],
        compiler_params=pltpu.CompilerParams(
            collective_id=1, has_side_effects=True, vmem_limit_bytes=60 * 2**20
        ),
    )(
        normed,
        d_out,
        w_qkv,
        w_out,
        block_order,
        jnp.asarray(frequency),
    )
    outs = [shape(1, rows, width)] * 2 + outs[2:]
    return pl.pallas_call(hand_on_kernel, out_shape=outs)(*results)


def solution(mesh):
    in_specs = (
        P("dp", "ctx", None),
        P(("dp", "ctx"), "tp"),
        P(("dp", "ctx"), "tp"),
        P(),
        P("dp", "ctx", None),
    )
    out_specs = (
        P("dp", "ctx", "tp"),
        P("dp", "ctx", "tp"),
        P(("dp", "ctx"), "tp"),
        P(("dp", "ctx"), "tp"),
    )
    return jax.shard_map(body, mesh=mesh, in_specs=in_specs, out_specs=out_specs, check_vma=False)
```

```python
import jax
import jax.numpy as jnp
import numpy as np
from jax import lax
from jax.experimental import pallas as pl
from jax.experimental.pallas import tpu as pltpu
from jax.sharding import PartitionSpec as P

HD = 128
SIDE = 4
MESH = pl.DeviceIdType.MESH

rope_base = 500000.0
masked_score = -1e30
contract_last = (((1,), (1,)), ((), ()))
contract_first = (((0,), (0,)), ((), ()))


class Links:
    def __init__(self, send, recv):
        self.send, self.recv, self.used, self.copies = send, recv, 0, []
        self.y = lax.axis_index("dp")
        self.c = lax.axis_index("ctx")
        self.t = lax.axis_index("tp")
        self.x = self.c // SIDE
        self.z = self.c % SIDE
        self.core = lax.rem(self.t, 2)
        self.side = self.t // 2

    def along_y(self, k):
        return (lax.rem(self.y + k, SIDE), self.c, self.t)

    def along_x(self, k):
        return (self.y, lax.rem(self.x + k, SIDE) * SIDE + self.z, self.t)

    def along_z(self, k):
        return (self.y, self.x * SIDE + lax.rem(self.z + k, SIDE), self.t)

    def other_core(self):
        return (self.y, self.c, self.t + 1 - 2 * self.core)

    def other_side(self):
        return (self.y, self.c, lax.rem(self.t + 2, 4))

    def greet(self):
        partners = (
            [self.along_y(k) for k in (1, 2, 3)]
            + [self.along_z(k) for k in (1, 2, 3)]
            + [self.along_x(1), self.along_x(3), self.other_core(), self.other_side()]
        )
        barrier = pltpu.get_barrier_semaphore()
        for partner in partners:
            pl.semaphore_signal(barrier, inc=1, device_id=partner, device_id_type=MESH)
        pl.semaphore_wait(barrier, len(partners))

    def copy(self, source, target, partner):
        made = pltpu.make_async_remote_copy(
            src_ref=source,
            dst_ref=target,
            send_sem=self.send.at[self.used],
            recv_sem=self.recv.at[self.used],
            device_id=partner,
            device_id_type=MESH,
        )
        made.start()
        self.used += 1
        self.copies.append(made)
        return made

    def finish(self):
        for made in self.copies:
            made.wait_send()


def local_copy(source, target, semaphore):
    made = pltpu.make_async_copy(source, target, semaphore)
    made.start()
    return made


def in_order(streams, order):
    for name in order:
        next(streams[name], None)


def to_end(streams):
    for stream in streams.values():
        for _ in stream:
            pass


def column(i, width=HD):
    return pl.ds(pl.multiple_of(i * width, width), width)


def ring_gather(links, along, here, view, arrived=None):
    before, after, across = (
        lax.rem(here + 3, SIDE),
        lax.rem(here + 1, SIDE),
        lax.rem(here + 2, SIDE),
    )
    arrived = arrived or (lambda block: None)
    own = view(here, None)
    right = links.copy(own, own, along(1))
    left = links.copy(own, own, along(3))
    yield
    right.wait_recv()
    passed = view(before, 0)
    onward = links.copy(passed, passed, along(1))
    left.wait_recv()
    passed = view(after, 1)
    back = links.copy(passed, passed, along(3))
    arrived(view(before, None))
    arrived(view(after, None))
    yield
    onward.wait_recv()
    arrived(view(across, 0))
    back.wait_recv()
    arrived(view(across, 1))


def gather_columns(links, source, chosen, full, first=0, count=None, x_first=False):
    y, x, z = links.y, links.x, links.z
    rows = pl.ds(first, count or source.shape[0])
    place = full.at[y, x, z, rows]
    copies = [
        links.copy(
            source.at[rows, column(chosen(lax.rem(y + k, SIDE)))], place, links.along_y(k)
        )
        for k in (2, 1, 3)
    ]
    yield
    for made in copies:
        made.wait_recv()
    if x_first:
        yield from ring_gather(
            links,
            links.along_x,
            x,
            lambda i, h: full.at[:, i, z] if h is None else full.at[pl.ds(2 * h, 2), i, z],
        )
        block = full.at[:, :, z]
    else:
        block = full.at[:, x, z, rows]
    copies = [links.copy(block, block, links.along_z(k)) for k in (2, 1, 3)]
    yield
    for made in copies:
        made.wait_recv()
    if not x_first:
        yield from ring_gather(
            links,
            links.along_x,
            x,
            lambda i, h: full.at[:, i, :, rows]
            if h is None
            else full.at[pl.ds(2 * h, 2), i, :, rows],
        )


def gather_tokens(links, full, handed):
    half = full.shape[1] // 2
    first = pl.multiple_of(links.core * half, half)

    def view(i, h):
        if h is None:
            return full.at[i, pl.ds(first, half)]
        return full.at[i, pl.ds(pl.multiple_of(first + h * (half // 2), half // 2), half // 2)]

    def hand(block):
        handed.append(links.copy(block, block, links.other_core()))

    yield from ring_gather(links, links.along_y, links.y, view, hand)
    yield
    for made in handed[2:]:
        made.wait_recv()


def gather_kind(links, full):
    x, z = links.x, links.z
    block = full.at[x, z]
    copies = [links.copy(block, block, links.along_z(k)) for k in (2, 1, 3)]
    yield
    for made in copies:
        made.wait_recv()
    yield from ring_gather(
        links,
        links.along_x,
        x,
        lambda i, h: full.at[i] if h is None else full.at[i, pl.ds(2 * h, 2)],
    )


def exchange_heads(links, source, place, own_semaphore):
    copies = [
        links.copy(source.at[lax.rem(links.y + k, SIDE)], place, links.along_y(k))
        for k in (2, 1, 3)
    ]
    return copies, local_copy(source.at[links.y], place, own_semaphore)


def add_blocks(target, *terms):
    lead, (height, width) = target.shape[:-2], target.shape[-2:]
    rows = min(height, max(16, 16384 // width))
    per = height // rows
    count = per
    for size in lead:
        count *= size

    def step(i, carry):
        at = (pl.ds(pl.multiple_of(i % per * rows, rows), rows),)
        rest = i // per
        for size in lead[::-1]:
            at = (rest % size,) + at
            rest = rest // size
        total = terms[0][at].astype(jnp.float32)
        for term in terms[1:]:
            total = total + term[at].astype(jnp.float32)
        target[at] = total.astype(target.dtype)
        return carry

    lax.fori_loop(0, count, step, 0)


def ring_sum(links, along, here, view, result, scratch, prepare=None, extra=None):
    passing, from_left, from_right = scratch
    left, right, across = (
        lax.rem(here + 3, SIDE),
        lax.rem(here + 1, SIDE),
        lax.rem(here + 2, SIDE),
    )
    prepare = prepare or (lambda i: None)
    extra = extra or (lambda h: ())
    prepare(across)
    first = links.copy(view(across, 0), passing.at[0], along(1))
    second = links.copy(view(across, 1), passing.at[1], along(3))
    prepare(right)
    plain_right = links.copy(view(right, 1), from_left.at[1], along(1))
    prepare(left)
    plain_left = links.copy(view(left, 0), from_right.at[0], along(3))
    yield
    prepare(here)
    first.wait_recv()
    add_blocks(passing.at[0], passing.at[0], view(right, 0))
    summed_right = links.copy(passing.at[0], from_left.at[0], along(1))
    second.wait_recv()
    add_blocks(passing.at[1], passing.at[1], view(left, 1))
    summed_left = links.copy(passing.at[1], from_right.at[1], along(3))
    yield
    plain_left.wait_recv()
    summed_right.wait_recv()
    add_blocks(result(0), view(here, 0), from_left.at[0], from_right.at[0], *extra(0))
    plain_right.wait_recv()
    summed_left.wait_recv()
    add_blocks(result(1), view(here, 1), from_left.at[1], from_right.at[1], *extra(1))


def sum_weight(links, tokens, grads, scratch):
    terms, ring, middle, arrived, summed, placed = scratch
    y, x, z = links.y, links.x, links.z
    size = 4 * terms.shape[3]

    def prepare(i):
        def step(owner, carry):
            at = column(owner * SIDE + i, size)
            rows = tokens[:, :, at].reshape(-1, size)
            part = lax.dot_general(
                rows,
                grads[...].reshape(rows.shape[0], HD),
                contract_first,
                preferred_element_type=jnp.float32,
            )
            terms[owner, i] = part.astype(jnp.bfloat16).reshape(terms.shape[2:])
            return carry

        lax.fori_loop(0, SIDE, step, 0)

    yield from ring_sum(
        links,
        links.along_x,
        x,
        lambda i, h: terms.at[pl.ds(2 * h, 2), i],
        lambda h: middle.at[pl.ds(2 * h, 2)],
        ring,
        prepare,
    )
    copies = [
        links.copy(middle.at[:, lax.rem(z + k, SIDE)], arrived.at[k - 1], links.along_z(k))
        for k in (2, 1, 3)
    ]
    yield
    for made in copies:
        made.wait_recv()
    add_blocks(summed, middle.at[:, z], arrived.at[0], arrived.at[1], arrived.at[2])
    copies = [
        links.copy(summed.at[lax.rem(y + k, SIDE)], placed.at[y], links.along_y(k))
        for k in (2, 1, 3)
    ]
    placed[y] = summed[y]
    yield
    for made in copies:
        made.wait_recv()


def sum_weight_scratch(rows):
    def vmem(*dims):
        return pltpu.VMEM(dims + (rows, HD), jnp.bfloat16)

    ring = (vmem(2, 2, 4), vmem(2, 2, 4), vmem(2, 2, 4))
    return (vmem(4, 4, 4), ring, vmem(4, 4), vmem(3, 4), vmem(4), vmem(4))


def sum_groups(links, rows, weight, result, start, scratch, own_part=None):
    terms, near, ring, paired, far = scratch
    whole, width = result.shape[1], terms.shape[3]
    core, side = links.core, links.side
    size = 256

    def prepare(owner):
        def step(i, carry):
            at = owner * (whole // size) + start // size + i
            part = lax.dot_general(
                rows[...].reshape(-1, HD),
                model_rows(weight, at, size),
                contract_last,
                preferred_element_type=jnp.float32,
            )
            terms[owner, :, :, column(i, size)] = part.astype(jnp.bfloat16).reshape(
                SIDE, rows.shape[1], size
            )
            return carry

        lax.fori_loop(0, width // size, step, 0)

    handed = []
    for i in range(2):
        prepare(2 * i + 1 - core)
        handed.append(links.copy(terms.at[2 * i + 1 - core], near.at[i], links.other_core()))
    for i in range(2):
        prepare(2 * i + core)
    yield
    for i in range(2):
        handed[i].wait_recv()
        add_blocks(terms.at[2 * i + core], terms.at[2 * i + core], near.at[i])
    yield from ring_sum(
        links,
        links.along_y,
        links.y,
        lambda i, h: terms.at[2 * h + core, i],
        lambda h: paired.at[h],
        ring,
        extra=None
        if own_part is None
        else lambda h: (own_part.at[2 * h + core, :, pl.ds(start, width)],),
    )
    across = links.copy(paired.at[1 - side], far, links.other_side())
    yield
    across.wait_recv()
    add_blocks(result.at[:, pl.ds(start, width)], paired.at[side], far)


def sum_groups_scratch(rows, width):
    def vmem(*dims):
        return pltpu.VMEM(dims + (rows, width), jnp.bfloat16)

    return (vmem(4, 4), vmem(2, 4), (vmem(2), vmem(2), vmem(2)), vmem(2), vmem())


def model_rows(weight, i, size):
    return weight[i // 4, i % 4].reshape(size, HD)


def own_groups(links, pieces, terms, near):
    core = links.core
    width, size = terms.shape[2], 256

    def prepare(owner):
        def step(i, carry):
            at = owner * (width // size) + i
            part = sum(
                lax.dot_general(
                    rows[...],
                    model_rows(weight, at, size),
                    contract_last,
                    preferred_element_type=jnp.float32,
                )
                for rows, weight in pieces
            )
            terms[owner, :, column(i, size)] = part.astype(jnp.bfloat16)
            return carry

        lax.fori_loop(0, width // size, step, 0)

    handed = []
    for i in range(2):
        prepare(2 * i + 1 - core)
        handed.append(links.copy(terms.at[2 * i + 1 - core], near.at[i], links.other_core()))
    for i in range(2):
        prepare(2 * i + core)
    yield
    for i in range(2):
        handed[i].wait_recv()
        add_blocks(terms.at[2 * i + core], terms.at[2 * i + core], near.at[i])


def sum_kind(links, terms, scratch):
    ring, middle, arrived, total = scratch
    x, z = links.x, links.z
    yield from ring_sum(
        links,
        links.along_x,
        x,
        lambda i, h: terms.at[i, pl.ds(2 * h, 2)],
        lambda h: middle.at[pl.ds(2 * h, 2)],
        ring,
    )
    copies = [
        links.copy(middle.at[lax.rem(z + k, SIDE)], arrived.at[k - 1], links.along_z(k))
        for k in (2, 1, 3)
    ]
    yield
    for made in copies:
        made.wait_recv()
    add_blocks(total, middle.at[z], arrived.at[0], arrived.at[1], arrived.at[2])


def sum_kind_scratch(rows):
    def vmem(*dims):
        return pltpu.VMEM(dims + (rows, HD), jnp.bfloat16)

    return ((vmem(2, 2), vmem(2, 2), vmem(2, 2)), vmem(4), vmem(3), pltpu.VMEM((rows, HD), jnp.float32))


def arrive(exchange):
    copies, own = exchange
    for made in copies:
        made.wait_recv()
    own.wait()


def hand_kv(links, key_total, value_total, cosine, sines, grads, handed):
    y = links.y
    key, value = key_total[...], value_total[...]
    key = key * cosine[...] - pltpu.roll(key, HD // 2, 1) * sines[...]
    keeps_key = lax.rem(y, 2) == 0
    handed[...] = jnp.where(keeps_key, value, key).astype(jnp.bfloat16)
    passed = links.copy(handed, grads.at[y, :, pl.ds(HD, HD)], links.along_y(3))
    grads[y, :, HD:] = jnp.where(keeps_key, key, value).astype(jnp.bfloat16)
    yield
    passed.wait_recv()


def project(sequences, weight, target):
    size = 1024

    def step(i, carry):
        part = jnp.dot(
            jnp.concatenate([tokens[:, column(i, size)] for tokens in sequences]),
            weight[i].reshape(size, HD),
            preferred_element_type=jnp.float32,
        ).reshape(target.shape)
        target[...] = jnp.where(i == 0, part, target[...] + part)
        return carry

    lax.fori_loop(0, SIDE, step, 0)


def attend(query_pos, key_pos, queries, kv, heads_out, raws, row_sums):
    to_power = HD ** (-0.5) * float(np.log2(np.e))
    length = key_pos.shape[0]
    pair = 2
    rows = pair * queries.shape[1]
    keys = kv[0].reshape(length, HD)
    values_t = kv[1].reshape(length, HD).T

    def step(i, carry):
        at = pl.ds(i * pair, pair)
        q = queries[at].reshape(rows, HD)
        allowed = key_pos[...] <= query_pos[...]
        scores = lax.dot_general(keys, q, contract_last, preferred_element_type=jnp.float32)
        scores = jnp.where(allowed, scores, masked_score)
        row_max = jnp.max(scores, axis=0, keepdims=True)
        raw = jnp.exp2((scores - row_max) * to_power)
        raws[i] = raw
        row_sum = jnp.sum(raw, axis=0, keepdims=True)
        row_sums[i] = row_sum
        weighted = jnp.dot(values_t, raw.astype(jnp.bfloat16), preferred_element_type=jnp.float32)
        heads_out[at] = (weighted / row_sum).T.astype(jnp.bfloat16).reshape(pair, -1, HD)
        return carry

    lax.fori_loop(0, queries.shape[0] // pair, step, 0)


def attend_back(
    i, cosine, sines, queries, head_grads, kv, heads_out, raws, row_sums, query_grad, totals
):
    score_scale = HD ** (-0.5)
    length = raws.shape[1]
    pair = 2
    rows = pair * queries.shape[1]
    keys_t = kv[0].reshape(length, HD).T
    values = kv[1].reshape(length, HD)
    turn = jnp.concatenate([cosine[...]] * pair), jnp.concatenate([sines[...]] * pair)
    at = pl.ds(i * pair, pair)
    q, grads = queries[at].reshape(rows, HD), head_grads[at].reshape(rows, HD)
    out = heads_out[at].reshape(rows, HD)
    row_dots = jnp.sum(
        (grads.astype(jnp.float32) * out.astype(jnp.float32)).T, axis=0, keepdims=True
    )
    weights = raws[i] * (1.0 / row_sums[i])
    dweights = lax.dot_general(values, grads, contract_last, preferred_element_type=jnp.float32)
    dscores = (weights * (dweights - row_dots)).astype(jnp.bfloat16)
    dq = jnp.dot(keys_t, dscores, preferred_element_type=jnp.float32).T * score_scale
    dq = dq * turn[0] - pltpu.roll(dq, HD // 2, 1) * turn[1]
    query_grad[at] = dq.astype(jnp.bfloat16).reshape(pair, -1, HD)
    key_part = jnp.dot(dscores, q, preferred_element_type=jnp.float32) * score_scale
    value_part = jnp.dot(
        weights.astype(jnp.bfloat16), grads, preferred_element_type=jnp.float32
    )
    totals[0] = key_part if i == 0 else totals[0] + key_part
    totals[1] = value_part if i == 0 else totals[1] + value_part


def place_tables(links, order, frequency, query_pos, key_pos, cosine, sines):
    rows = cosine.shape[0]
    block = rows // 2
    first, second = order[2 * links.c] * block, order[2 * links.c + 1] * block

    def positions(dims, axis):
        row = lax.rem(lax.broadcasted_iota(jnp.int32, dims, axis), rows)
        return jnp.where(row < block, first, second - block) + row

    query_pos[...] = positions(query_pos.shape, 1)
    angles = positions(cosine.shape, 0).astype(jnp.float32) * frequency[...]
    lane = lax.broadcasted_iota(jnp.int32, sines.shape, 1)
    sine = jnp.sin(angles)
    cosine[...] = jnp.cos(angles)
    sines[...] = jnp.where(lane < HD // 2, -sine, sine)
    row = lax.broadcasted_iota(jnp.int32, (block, 1), 0)
    for i in range(key_pos.shape[0] // block):
        key_pos[i * block : (i + 1) * block] = order[i] * block + row


FRONT = "joqknjdkjqknjkoqkoqjPvPVdvKonqvVKnQoVvdKdGKV"
BACK = "ABBYXabaYsXfYaXrfbagvfYbXhgrubhwursgwfrsawgbsgrwswf"


def whole_kernel(
    normed, d_out, w_qkv, w_out, order, frequency,
    attn_out, d_normed, d_w_qkv, d_w_out,
    tables, tokens, weights, blocks, wide, rows_kv, own, sums, send, recv, local,
):
    links = Links(send, recv)
    y, x, z = links.y, links.x, links.z
    heads = w_out.shape[1] // HD
    query_pos, key_pos, cosine, sines = tables
    all_normed, all_d_out = tokens
    full_q, full_kv, full_out, full_other = weights
    my_queries, my_grads, queries, head_grads, heads_out, query_grad, all_heads = blocks
    projected, grads = wide
    my_kv, all_kv, totals, kv_terms, handed, raws, row_sums = rows_kv
    after = lax.rem(y + 1, SIDE)

    given = {
        "k": (w_qkv, lambda j: heads + lax.rem(j, 2), full_kv),
        "q": (w_qkv, lambda j: j, full_q),
        "o": (w_out, lambda j: j, full_out),
        "v": (w_qkv, lambda j: heads + lax.rem(j + 1, 2), full_other),
    }
    mine = [
        local_copy(source.at[:, column(chosen(y))], full.at[y, x, z], local.at[i])
        for i, (source, chosen, full) in enumerate(given.values())
    ]
    mine += [
        local_copy(source.at[0], full.at[y], local.at[4 + i])
        for i, (source, full) in enumerate(((normed, all_normed), (d_out, all_d_out)))
    ]
    for k in (2, 3):
        grads[lax.rem(y + k, SIDE), :, HD:] = jnp.zeros_like(grads[0, :, HD:])
    links.greet()
    streams = {name: gather_columns(links, *given[name]) for name in "qo"}
    half = w_qkv.shape[0] // 2
    streams["k"] = gather_columns(links, *given["k"], 0, half)
    streams["j"] = gather_columns(links, *given["k"], half, half)
    streams["v"] = gather_columns(links, *given["v"], x_first=True)
    handed_n, handed_d = [], []
    streams["n"] = gather_tokens(links, all_normed, handed_n)
    streams["d"] = gather_tokens(links, all_d_out, handed_d)
    for made in mine:
        made.wait()
    in_order(streams, FRONT[:9])
    place_tables(links, order, frequency, query_pos, key_pos, cosine, sines)
    held = {}

    def project_kv():
        for made in handed_n[:2]:
            made.wait_recv()
        project([all_normed.at[y], all_normed.at[after]], full_kv, projected.at[pl.ds(0, 2)])
        for i in range(2):
            part = projected[i]
            turned = part * cosine[...] + pltpu.roll(part, HD // 2, 1) * sines[...]
            my_kv[i] = jnp.where(lax.rem(y, 2) == 0, turned, part).astype(jnp.bfloat16)
        place = all_kv.at[lax.rem(y, 2), x, z]
        passed = links.copy(my_kv.at[1], place, links.along_y(1))
        place[...] = my_kv[0]
        yield
        passed.wait_recv()

    def project_queries():
        project([all_normed.at[i] for i in range(SIDE)], full_q, projected)
        for i in range(SIDE):
            part = projected[i]
            turned = part * cosine[...] + pltpu.roll(part, HD // 2, 1) * sines[...]
            my_queries[i] = turned.astype(jnp.bfloat16)
        held["Q"] = exchange_heads(links, my_queries, queries.at[y], local.at[0])
        yield

    def project_grads():
        for made in handed_d[:2]:
            made.wait_recv()
        project([all_d_out.at[i] for i in range(SIDE)], full_out, projected)
        my_grads[...] = projected[...].astype(jnp.bfloat16)
        held["G"] = exchange_heads(links, my_grads, head_grads.at[y], local.at[1])
        yield

    streams["P"] = project_kv()
    streams["Q"] = project_queries()
    streams["G"] = project_grads()
    streams["K"] = gather_kind(links, all_kv.at[0])
    streams["V"] = gather_kind(links, all_kv.at[1])

    def attend_forward():
        arrive(held.pop("Q"))
        attend(query_pos, key_pos, queries, all_kv, heads_out, raws, row_sums)
        held["heads"] = exchange_heads(links, heads_out, all_heads.at[y], local.at[0])
        yield

    def attend_backward():
        arrive(held.pop("G"))
        for i in range(2):
            attend_back(
                i, cosine, sines, queries, head_grads, all_kv, heads_out, raws, row_sums,
                query_grad, totals,
            )
            if i == 0:
                yield
        kv_terms[...] = totals[...].astype(jnp.bfloat16).reshape(kv_terms.shape)
        held["grads"] = exchange_heads(
            links, query_grad, grads.at[y, :, pl.ds(0, HD)], local.at[1]
        )
        yield

    streams["A"] = attend_forward()
    streams["B"] = attend_backward()

    def having(name, stream):
        if name in held:
            arrive(held.pop(name))
        yield from stream

    half = sums[2][0].shape[3]
    own_terms, own_near = own
    query_part, kv_part = grads.at[:, :, pl.ds(0, HD)], grads.at[:, :, pl.ds(HD, HD)]
    own_pieces = [(grads.at[y, :, pl.ds(HD, HD)], full_kv), (handed, full_other)]
    streams["X"] = sum_kind(links, kv_terms.at[0], sums[0])
    streams["Y"] = sum_kind(links, kv_terms.at[1], sums[1])
    streams["h"] = hand_kv(links, sums[0][3], sums[1][3], cosine, sines, grads, handed)
    streams["u"] = own_groups(links, own_pieces, own_terms, own_near)
    streams["w"] = sum_weight(links, all_normed, kv_part, sums[8])
    for name, needs, stream in (
        ("a", "heads", sum_groups(links, all_heads, full_out, attn_out, 0, sums[2])),
        ("b", "heads", sum_groups(links, all_heads, full_out, attn_out, half, sums[3])),
        ("r", "grads", sum_groups(links, query_part, full_q, d_normed, 0, sums[4], own_terms)),
        ("s", "grads", sum_groups(links, query_part, full_q, d_normed, half, sums[5], own_terms)),
        ("f", "heads", sum_weight(links, all_d_out, all_heads, sums[6])),
        ("g", "grads", sum_weight(links, all_normed, query_part, sums[7])),
    ):
        streams[name] = having(needs, stream)
    in_order(streams, FRONT[9:] + BACK)
    to_end(streams)
    links.finish()
    placed_out, placed_q, placed_kv = sums[6][5], sums[7][5], sums[8][5]
    width = SIDE * HD
    for j in range(SIDE):
        d_w_out[:, j * HD : (j + 1) * HD] = placed_out[j]
        d_w_qkv[:, j * HD : (j + 1) * HD] = placed_q[j]
    for kind in range(2):
        total = placed_kv[kind].astype(jnp.float32) + placed_kv[kind + 2].astype(jnp.float32)
        d_w_qkv[:, width + kind * HD : width + (kind + 1) * HD] = total.astype(jnp.bfloat16)


def hand_on_kernel(*refs):
    half = len(refs) // 2
    for source, target in zip(refs[:half], refs[half:]):
        target[...] = source[...].reshape(target.shape)


VMEM = pl.BlockSpec(memory_space=pltpu.VMEM)
HBM = pl.BlockSpec(memory_space=pl.ANY)


def shape(*dims):
    return jax.ShapeDtypeStruct(dims, jnp.bfloat16)


def body(normed, w_qkv, w_out, block_order, d_out):
    rows, model = normed.shape[1], normed.shape[2]
    part = w_out.shape[0]
    length = rows * lax.axis_size("ctx")
    frequency = rope_base ** (-2.0 * np.arange(HD // 2, dtype=np.float64) / HD)
    frequency = np.tile(frequency, 2).astype(np.float32)[None, :]
    width = model // 4

    def vmem(*dims, kind=jnp.bfloat16):
        return pltpu.VMEM(dims, kind)

    blocks = vmem(4, rows, HD)
    copies = 5 * 10 + 2 * 8 + 1 + 2 * 7 + 4 * 3 + 2 * 9 + 1 + 2 + 4 * 9 + 3 * 12
    outs = [shape(rows, width), shape(rows, width), shape(*w_qkv.shape), shape(*w_out.shape)]
    results = pl.pallas_call(
        whole_kernel,
        out_shape=outs,
        in_specs=[HBM] * 4 + [pl.BlockSpec(memory_space=pltpu.SMEM), VMEM],
        out_specs=[VMEM] * 4,
        scratch_shapes=[
            (
                vmem(1, 2 * rows, kind=jnp.int32),
                vmem(length, 1, kind=jnp.int32),
                vmem(rows, HD, kind=jnp.float32),
                vmem(rows, HD, kind=jnp.float32),
            ),
            (vmem(4, rows, model),) * 2,
            (vmem(4, 4, 4, part, HD),) * 4,
            (blocks,) * 7,
            (vmem(4, rows, HD, kind=jnp.float32), vmem(4, rows, 2 * HD)),
            (
                vmem(2, rows, HD),
                vmem(2, 4, 4, rows, HD),
                vmem(2, length, HD, kind=jnp.float32),
                vmem(2, 4, 4, rows, HD),
                vmem(rows, HD),
                vmem(2, length, 2 * rows, kind=jnp.float32),
                vmem(2, 1, 2 * rows, kind=jnp.float32),
            ),
            (vmem(4, rows, width), vmem(2, rows, width)),
            (sum_kind_scratch(rows),) * 2
            + (sum_groups_scratch(rows, width // 2),) * 4
            + (sum_weight_scratch(part),) * 3,
            pltpu.SemaphoreType.DMA((copies,)),
            pltpu.SemaphoreType.DMA((copies,)),
            pltpu.SemaphoreType.DMA((6,)),
        ],
        compiler_params=pltpu.CompilerParams(
            collective_id=1, has_side_effects=True, vmem_limit_bytes=60 * 2**20
        ),
    )(
        normed,
        d_out,
        w_qkv,
        w_out,
        block_order,
        jnp.asarray(frequency),
    )
    outs = [shape(1, rows, width)] * 2 + outs[2:]
    return pl.pallas_call(hand_on_kernel, out_shape=outs)(*results)


def solution(mesh):
    in_specs = (
        P("dp", "ctx", None),
        P(("dp", "ctx"), "tp"),
        P(("dp", "ctx"), "tp"),
        P(),
        P("dp", "ctx", None),
    )
    out_specs = (
        P("dp", "ctx", "tp"),
        P("dp", "ctx", "tp"),
        P(("dp", "ctx"), "tp"),
        P(("dp", "ctx"), "tp"),
    )
    return jax.shard_map(body, mesh=mesh, in_specs=in_specs, out_specs=out_specs, check_vma=False)
```

```python
import jax
import jax.numpy as jnp
import numpy as np
from jax import lax
from jax.experimental import pallas as pl
from jax.experimental.pallas import tpu as pltpu
from jax.sharding import PartitionSpec as P

HD = 128
SIDE = 4
MESH = pl.DeviceIdType.MESH

rope_base = 500000.0
masked_score = -1e30
contract_last = (((1,), (1,)), ((), ()))
contract_first = (((0,), (0,)), ((), ()))


class Links:
    def __init__(self, send, recv):
        self.send, self.recv, self.used, self.copies = send, recv, 0, []
        self.y = lax.axis_index("dp")
        self.c = lax.axis_index("ctx")
        self.t = lax.axis_index("tp")
        self.x = self.c // SIDE
        self.z = self.c % SIDE
        self.core = lax.rem(self.t, 2)
        self.side = self.t // 2

    def along_y(self, k):
        return (lax.rem(self.y + k, SIDE), self.c, self.t)

    def along_x(self, k):
        return (self.y, lax.rem(self.x + k, SIDE) * SIDE + self.z, self.t)

    def along_z(self, k):
        return (self.y, self.x * SIDE + lax.rem(self.z + k, SIDE), self.t)

    def other_core(self):
        return (self.y, self.c, self.t + 1 - 2 * self.core)

    def other_side(self):
        return (self.y, self.c, lax.rem(self.t + 2, 4))

    def greet(self):
        partners = (
            [self.along_y(k) for k in (1, 2, 3)]
            + [self.along_z(k) for k in (1, 2, 3)]
            + [self.along_x(1), self.along_x(3), self.other_core(), self.other_side()]
        )
        barrier = pltpu.get_barrier_semaphore()
        for partner in partners:
            pl.semaphore_signal(barrier, inc=1, device_id=partner, device_id_type=MESH)
        pl.semaphore_wait(barrier, len(partners))

    def copy(self, source, target, partner):
        made = pltpu.make_async_remote_copy(
            src_ref=source,
            dst_ref=target,
            send_sem=self.send.at[self.used],
            recv_sem=self.recv.at[self.used],
            device_id=partner,
            device_id_type=MESH,
        )
        made.start()
        self.used += 1
        self.copies.append(made)
        return made

    def finish(self):
        for made in self.copies:
            made.wait_send()


def local_copy(source, target, semaphore):
    made = pltpu.make_async_copy(source, target, semaphore)
    made.start()
    return made


def in_order(streams, order):
    for name in order:
        next(streams[name], None)


def to_end(streams):
    for stream in streams.values():
        for _ in stream:
            pass


def column(i, width=HD):
    return pl.ds(pl.multiple_of(i * width, width), width)


def ring_gather(links, along, here, view, arrived=None):
    before, after, across = (
        lax.rem(here + 3, SIDE),
        lax.rem(here + 1, SIDE),
        lax.rem(here + 2, SIDE),
    )
    arrived = arrived or (lambda block: None)
    own = view(here, None)
    right = links.copy(own, own, along(1))
    left = links.copy(own, own, along(3))
    yield
    right.wait_recv()
    passed = view(before, 0)
    onward = links.copy(passed, passed, along(1))
    left.wait_recv()
    passed = view(after, 1)
    back = links.copy(passed, passed, along(3))
    arrived(view(before, None))
    arrived(view(after, None))
    yield
    onward.wait_recv()
    arrived(view(across, 0))
    back.wait_recv()
    arrived(view(across, 1))


def gather_columns(links, source, chosen, full, first=0, count=None, x_first=False):
    y, x, z = links.y, links.x, links.z
    rows = pl.ds(first, count or source.shape[0])
    place = full.at[y, x, z, rows]
    copies = [
        links.copy(
            source.at[rows, column(chosen(lax.rem(y + k, SIDE)))], place, links.along_y(k)
        )
        for k in (2, 1, 3)
    ]
    yield
    for made in copies:
        made.wait_recv()
    if x_first:
        yield from ring_gather(
            links,
            links.along_x,
            x,
            lambda i, h: full.at[:, i, z] if h is None else full.at[pl.ds(2 * h, 2), i, z],
        )
        block = full.at[:, :, z]
    else:
        block = full.at[:, x, z, rows]
    copies = [links.copy(block, block, links.along_z(k)) for k in (2, 1, 3)]
    yield
    for made in copies:
        made.wait_recv()
    if not x_first:
        yield from ring_gather(
            links,
            links.along_x,
            x,
            lambda i, h: full.at[:, i, :, rows]
            if h is None
            else full.at[pl.ds(2 * h, 2), i, :, rows],
        )


def gather_tokens(links, full, handed):
    half = full.shape[1] // 2
    first = pl.multiple_of(links.core * half, half)

    def view(i, h):
        if h is None:
            return full.at[i, pl.ds(first, half)]
        return full.at[i, pl.ds(pl.multiple_of(first + h * (half // 2), half // 2), half // 2)]

    def hand(block):
        handed.append(links.copy(block, block, links.other_core()))

    yield from ring_gather(links, links.along_y, links.y, view, hand)
    yield
    for made in handed[2:]:
        made.wait_recv()


def gather_kind(links, full):
    x, z = links.x, links.z
    block = full.at[x, z]
    copies = [links.copy(block, block, links.along_z(k)) for k in (2, 1, 3)]
    yield
    for made in copies:
        made.wait_recv()
    yield from ring_gather(
        links,
        links.along_x,
        x,
        lambda i, h: full.at[i] if h is None else full.at[i, pl.ds(2 * h, 2)],
    )


def exchange_heads(links, source, place, own_semaphore):
    copies = [
        links.copy(source.at[lax.rem(links.y + k, SIDE)], place, links.along_y(k))
        for k in (2, 1, 3)
    ]
    return copies, local_copy(source.at[links.y], place, own_semaphore)


def add_blocks(target, *terms):
    lead, (height, width) = target.shape[:-2], target.shape[-2:]
    rows = min(height, max(16, 16384 // width))
    per = height // rows
    count = per
    for size in lead:
        count *= size

    def step(i, carry):
        at = (pl.ds(pl.multiple_of(i % per * rows, rows), rows),)
        rest = i // per
        for size in lead[::-1]:
            at = (rest % size,) + at
            rest = rest // size
        total = terms[0][at].astype(jnp.float32)
        for term in terms[1:]:
            total = total + term[at].astype(jnp.float32)
        target[at] = total.astype(target.dtype)
        return carry

    lax.fori_loop(0, count, step, 0)


def ring_sum(links, along, here, view, result, scratch, prepare=None, extra=None):
    passing, from_left, from_right = scratch
    left, right, across = (
        lax.rem(here + 3, SIDE),
        lax.rem(here + 1, SIDE),
        lax.rem(here + 2, SIDE),
    )
    prepare = prepare or (lambda i: None)
    extra = extra or (lambda h: ())
    prepare(across)
    first = links.copy(view(across, 0), passing.at[0], along(1))
    second = links.copy(view(across, 1), passing.at[1], along(3))
    prepare(right)
    plain_right = links.copy(view(right, 1), from_left.at[1], along(1))
    prepare(left)
    plain_left = links.copy(view(left, 0), from_right.at[0], along(3))
    yield
    prepare(here)
    first.wait_recv()
    add_blocks(passing.at[0], passing.at[0], view(right, 0))
    summed_right = links.copy(passing.at[0], from_left.at[0], along(1))
    second.wait_recv()
    add_blocks(passing.at[1], passing.at[1], view(left, 1))
    summed_left = links.copy(passing.at[1], from_right.at[1], along(3))
    yield
    plain_left.wait_recv()
    summed_right.wait_recv()
    add_blocks(result(0), view(here, 0), from_left.at[0], from_right.at[0], *extra(0))
    plain_right.wait_recv()
    summed_left.wait_recv()
    add_blocks(result(1), view(here, 1), from_left.at[1], from_right.at[1], *extra(1))


def sum_weight(links, tokens, grads, scratch):
    terms, ring, middle, arrived, passed, summed, placed = scratch
    y, x, z = links.y, links.x, links.z
    size = 4 * terms.shape[3]

    def prepare(i):
        def step(owner, carry):
            at = column(owner * SIDE + i, size)
            rows = tokens[:, :, at].reshape(-1, size)
            part = lax.dot_general(
                rows,
                grads[...].reshape(rows.shape[0], HD),
                contract_first,
                preferred_element_type=jnp.float32,
            )
            terms[owner, i] = part.astype(jnp.bfloat16).reshape(terms.shape[2:])
            return carry

        lax.fori_loop(0, SIDE, step, 0)

    yield from ring_sum(
        links,
        links.along_x,
        x,
        lambda i, h: terms.at[pl.ds(2 * h, 2), i],
        lambda h: middle.at[pl.ds(2 * h, 2)],
        ring,
        prepare,
    )
    step = 1 + 2 * lax.rem(z, 2)
    neighbour, other = lax.rem(z + step, SIDE), lax.rem(z + 2, SIDE)
    first = links.copy(
        middle.at[:, lax.rem(neighbour + 2, SIDE)], arrived.at[0], links.along_z(step)
    )
    second = links.copy(middle.at[:, neighbour], arrived.at[1], links.along_z(step))
    yield
    first.wait_recv()
    add_blocks(passed, middle.at[:, other], arrived.at[0])
    third = links.copy(passed, arrived.at[2], links.along_z(2))
    yield
    second.wait_recv()
    third.wait_recv()
    add_blocks(summed, middle.at[:, z], arrived.at[1], arrived.at[2])
    copies = [
        links.copy(summed.at[lax.rem(y + k, SIDE)], placed.at[y], links.along_y(k))
        for k in (2, 1, 3)
    ]
    placed[y] = summed[y]
    yield
    for made in copies:
        made.wait_recv()


def sum_weight_scratch(rows):
    def vmem(*dims):
        return pltpu.VMEM(dims + (rows, HD), jnp.bfloat16)

    ring = (vmem(2, 2, 4), vmem(2, 2, 4), vmem(2, 2, 4))
    return (vmem(4, 4, 4), ring, vmem(4, 4), vmem(3, 4), vmem(4), vmem(4), vmem(4))


def sum_groups(links, rows, weight, result, start, scratch, own_part=None):
    terms, near, ring, paired, far = scratch
    whole, width = result.shape[1], terms.shape[3]
    core, side = links.core, links.side
    size = 256

    def prepare(owner):
        def step(i, carry):
            at = owner * (whole // size) + start // size + i
            part = lax.dot_general(
                rows[...].reshape(-1, HD),
                model_rows(weight, at, size),
                contract_last,
                preferred_element_type=jnp.float32,
            )
            terms[owner, :, :, column(i, size)] = part.astype(jnp.bfloat16).reshape(
                SIDE, rows.shape[1], size
            )
            return carry

        lax.fori_loop(0, width // size, step, 0)

    handed = []
    for i in range(2):
        prepare(2 * i + 1 - core)
        handed.append(links.copy(terms.at[2 * i + 1 - core], near.at[i], links.other_core()))
    for i in range(2):
        prepare(2 * i + core)
    yield
    for i in range(2):
        handed[i].wait_recv()
        add_blocks(terms.at[2 * i + core], terms.at[2 * i + core], near.at[i])
    yield from ring_sum(
        links,
        links.along_y,
        links.y,
        lambda i, h: terms.at[2 * h + core, i],
        lambda h: paired.at[h],
        ring,
        extra=None
        if own_part is None
        else lambda h: (own_part.at[2 * h + core, :, pl.ds(start, width)],),
    )
    across = links.copy(paired.at[1 - side], far, links.other_side())
    yield
    across.wait_recv()
    add_blocks(result.at[:, pl.ds(start, width)], paired.at[side], far)


def sum_groups_scratch(rows, width):
    def vmem(*dims):
        return pltpu.VMEM(dims + (rows, width), jnp.bfloat16)

    return (vmem(4, 4), vmem(2, 4), (vmem(2), vmem(2), vmem(2)), vmem(2), vmem())


def model_rows(weight, i, size):
    return weight[i // 4, i % 4].reshape(size, HD)


def own_groups(links, pieces, terms, near):
    core = links.core
    width, size = terms.shape[2], 256

    def prepare(owner):
        def step(i, carry):
            at = owner * (width // size) + i
            part = sum(
                lax.dot_general(
                    rows[...],
                    model_rows(weight, at, size),
                    contract_last,
                    preferred_element_type=jnp.float32,
                )
                for rows, weight in pieces
            )
            terms[owner, :, column(i, size)] = part.astype(jnp.bfloat16)
            return carry

        lax.fori_loop(0, width // size, step, 0)

    handed = []
    for i in range(2):
        prepare(2 * i + 1 - core)
        handed.append(links.copy(terms.at[2 * i + 1 - core], near.at[i], links.other_core()))
    for i in range(2):
        prepare(2 * i + core)
    yield
    for i in range(2):
        handed[i].wait_recv()
        add_blocks(terms.at[2 * i + core], terms.at[2 * i + core], near.at[i])


def sum_kind(links, terms, scratch):
    ring, middle, arrived, total = scratch
    x, z = links.x, links.z
    yield from ring_sum(
        links,
        links.along_x,
        x,
        lambda i, h: terms.at[i, pl.ds(2 * h, 2)],
        lambda h: middle.at[pl.ds(2 * h, 2)],
        ring,
    )
    copies = [
        links.copy(middle.at[lax.rem(z + k, SIDE)], arrived.at[k - 1], links.along_z(k))
        for k in (2, 1, 3)
    ]
    yield
    for made in copies:
        made.wait_recv()
    add_blocks(total, middle.at[z], arrived.at[0], arrived.at[1], arrived.at[2])


def sum_kind_scratch(rows):
    def vmem(*dims):
        return pltpu.VMEM(dims + (rows, HD), jnp.bfloat16)

    return ((vmem(2, 2), vmem(2, 2), vmem(2, 2)), vmem(4), vmem(3), pltpu.VMEM((rows, HD), jnp.float32))


def arrive(exchange):
    copies, own = exchange
    for made in copies:
        made.wait_recv()
    own.wait()


def hand_kv(links, key_total, value_total, cosine, sines, grads, handed):
    y = links.y
    key, value = key_total[...], value_total[...]
    key = key * cosine[...] - pltpu.roll(key, HD // 2, 1) * sines[...]
    keeps_key = lax.rem(y, 2) == 0
    handed[...] = jnp.where(keeps_key, value, key).astype(jnp.bfloat16)
    passed = links.copy(handed, grads.at[y, :, pl.ds(HD, HD)], links.along_y(3))
    grads[y, :, HD:] = jnp.where(keeps_key, key, value).astype(jnp.bfloat16)
    yield
    passed.wait_recv()


def project(sequences, weight, target):
    size = 1024

    def step(i, carry):
        part = jnp.dot(
            jnp.concatenate([tokens[:, column(i, size)] for tokens in sequences]),
            weight[i].reshape(size, HD),
            preferred_element_type=jnp.float32,
        ).reshape(target.shape)
        target[...] = jnp.where(i == 0, part, target[...] + part)
        return carry

    lax.fori_loop(0, SIDE, step, 0)


def attend(query_pos, key_pos, queries, kv, heads_out, raws, row_sums):
    to_power = HD ** (-0.5) * float(np.log2(np.e))
    length = key_pos.shape[0]
    pair = 2
    rows = pair * queries.shape[1]
    keys = kv[0].reshape(length, HD)
    values_t = kv[1].reshape(length, HD).T

    def step(i, carry):
        at = pl.ds(i * pair, pair)
        q = queries[at].reshape(rows, HD)
        allowed = key_pos[...] <= query_pos[...]
        scores = lax.dot_general(keys, q, contract_last, preferred_element_type=jnp.float32)
        scores = jnp.where(allowed, scores, masked_score)
        row_max = jnp.max(scores, axis=0, keepdims=True)
        raw = jnp.exp2((scores - row_max) * to_power)
        raws[i] = raw
        row_sum = jnp.sum(raw, axis=0, keepdims=True)
        row_sums[i] = row_sum
        weighted = jnp.dot(values_t, raw.astype(jnp.bfloat16), preferred_element_type=jnp.float32)
        heads_out[at] = (weighted / row_sum).T.astype(jnp.bfloat16).reshape(pair, -1, HD)
        return carry

    lax.fori_loop(0, queries.shape[0] // pair, step, 0)


def attend_back(
    i, cosine, sines, queries, head_grads, kv, heads_out, raws, row_sums, query_grad, totals
):
    score_scale = HD ** (-0.5)
    length = raws.shape[1]
    pair = 2
    rows = pair * queries.shape[1]
    keys_t = kv[0].reshape(length, HD).T
    values = kv[1].reshape(length, HD)
    turn = jnp.concatenate([cosine[...]] * pair), jnp.concatenate([sines[...]] * pair)
    at = pl.ds(i * pair, pair)
    q, grads = queries[at].reshape(rows, HD), head_grads[at].reshape(rows, HD)
    out = heads_out[at].reshape(rows, HD)
    row_dots = jnp.sum(
        (grads.astype(jnp.float32) * out.astype(jnp.float32)).T, axis=0, keepdims=True
    )
    weights = raws[i] * (1.0 / row_sums[i])
    dweights = lax.dot_general(values, grads, contract_last, preferred_element_type=jnp.float32)
    dscores = (weights * (dweights - row_dots)).astype(jnp.bfloat16)
    dq = jnp.dot(keys_t, dscores, preferred_element_type=jnp.float32).T * score_scale
    dq = dq * turn[0] - pltpu.roll(dq, HD // 2, 1) * turn[1]
    query_grad[at] = dq.astype(jnp.bfloat16).reshape(pair, -1, HD)
    key_part = jnp.dot(dscores, q, preferred_element_type=jnp.float32) * score_scale
    value_part = jnp.dot(
        weights.astype(jnp.bfloat16), grads, preferred_element_type=jnp.float32
    )
    totals[0] = key_part if i == 0 else totals[0] + key_part
    totals[1] = value_part if i == 0 else totals[1] + value_part


def place_tables(links, order, frequency, query_pos, key_pos, cosine, sines):
    rows = cosine.shape[0]
    block = rows // 2
    first, second = order[2 * links.c] * block, order[2 * links.c + 1] * block

    def positions(dims, axis):
        row = lax.rem(lax.broadcasted_iota(jnp.int32, dims, axis), rows)
        return jnp.where(row < block, first, second - block) + row

    query_pos[...] = positions(query_pos.shape, 1)
    angles = positions(cosine.shape, 0).astype(jnp.float32) * frequency[...]
    lane = lax.broadcasted_iota(jnp.int32, sines.shape, 1)
    sine = jnp.sin(angles)
    cosine[...] = jnp.cos(angles)
    sines[...] = jnp.where(lane < HD // 2, -sine, sine)
    row = lax.broadcasted_iota(jnp.int32, (block, 1), 0)
    for i in range(key_pos.shape[0] // block):
        key_pos[i * block : (i + 1) * block] = order[i] * block + row


FRONT = "kqojnkdjokjjkqonjkPqovdqPKvVnKqVvnQdKVovdGKV"
BACK = "ABBXYbabXYgbYXagrbvfaYXhgrfuahwsfrwugsafwgrsbwsrwgfsfw"


def whole_kernel(
    normed, d_out, w_qkv, w_out, order, frequency,
    attn_out, d_normed, d_w_qkv, d_w_out,
    tables, tokens, weights, blocks, wide, rows_kv, own, sums, send, recv, local,
):
    links = Links(send, recv)
    y, x, z = links.y, links.x, links.z
    heads = w_out.shape[1] // HD
    query_pos, key_pos, cosine, sines = tables
    all_normed, all_d_out = tokens
    full_q, full_kv, full_out, full_other = weights
    my_queries, my_grads, queries, head_grads, heads_out, query_grad, all_heads = blocks
    projected, grads = wide
    my_kv, all_kv, totals, kv_terms, handed, raws, row_sums = rows_kv
    after = lax.rem(y + 1, SIDE)

    given = {
        "k": (w_qkv, lambda j: heads + lax.rem(j, 2), full_kv),
        "q": (w_qkv, lambda j: j, full_q),
        "o": (w_out, lambda j: j, full_out),
        "v": (w_qkv, lambda j: heads + lax.rem(j + 1, 2), full_other),
    }
    mine = [
        local_copy(source.at[:, column(chosen(y))], full.at[y, x, z], local.at[i])
        for i, (source, chosen, full) in enumerate(given.values())
    ]
    mine += [
        local_copy(source.at[0], full.at[y], local.at[4 + i])
        for i, (source, full) in enumerate(((normed, all_normed), (d_out, all_d_out)))
    ]
    for k in (2, 3):
        grads[lax.rem(y + k, SIDE), :, HD:] = jnp.zeros_like(grads[0, :, HD:])
    links.greet()
    streams = {name: gather_columns(links, *given[name]) for name in "qo"}
    half = w_qkv.shape[0] // 2
    streams["k"] = gather_columns(links, *given["k"], 0, half)
    streams["j"] = gather_columns(links, *given["k"], half, half)
    streams["v"] = gather_columns(links, *given["v"], x_first=True)
    handed_n, handed_d = [], []
    streams["n"] = gather_tokens(links, all_normed, handed_n)
    streams["d"] = gather_tokens(links, all_d_out, handed_d)
    for made in mine:
        made.wait()
    in_order(streams, FRONT[:9])
    place_tables(links, order, frequency, query_pos, key_pos, cosine, sines)
    held = {}

    def project_kv():
        for made in handed_n[:2]:
            made.wait_recv()
        project([all_normed.at[y], all_normed.at[after]], full_kv, projected.at[pl.ds(0, 2)])
        for i in range(2):
            part = projected[i]
            turned = part * cosine[...] + pltpu.roll(part, HD // 2, 1) * sines[...]
            my_kv[i] = jnp.where(lax.rem(y, 2) == 0, turned, part).astype(jnp.bfloat16)
        place = all_kv.at[lax.rem(y, 2), x, z]
        passed = links.copy(my_kv.at[1], place, links.along_y(1))
        place[...] = my_kv[0]
        yield
        passed.wait_recv()

    def project_queries():
        project([all_normed.at[i] for i in range(SIDE)], full_q, projected)
        for i in range(SIDE):
            part = projected[i]
            turned = part * cosine[...] + pltpu.roll(part, HD // 2, 1) * sines[...]
            my_queries[i] = turned.astype(jnp.bfloat16)
        held["Q"] = exchange_heads(links, my_queries, queries.at[y], local.at[0])
        yield

    def project_grads():
        for made in handed_d[:2]:
            made.wait_recv()
        project([all_d_out.at[i] for i in range(SIDE)], full_out, projected)
        my_grads[...] = projected[...].astype(jnp.bfloat16)
        held["G"] = exchange_heads(links, my_grads, head_grads.at[y], local.at[1])
        yield

    streams["P"] = project_kv()
    streams["Q"] = project_queries()
    streams["G"] = project_grads()
    streams["K"] = gather_kind(links, all_kv.at[0])
    streams["V"] = gather_kind(links, all_kv.at[1])

    def attend_forward():
        arrive(held.pop("Q"))
        attend(query_pos, key_pos, queries, all_kv, heads_out, raws, row_sums)
        held["heads"] = exchange_heads(links, heads_out, all_heads.at[y], local.at[0])
        yield

    def attend_backward():
        arrive(held.pop("G"))
        for i in range(2):
            attend_back(
                i, cosine, sines, queries, head_grads, all_kv, heads_out, raws, row_sums,
                query_grad, totals,
            )
            if i == 0:
                yield
        kv_terms[...] = totals[...].astype(jnp.bfloat16).reshape(kv_terms.shape)
        held["grads"] = exchange_heads(
            links, query_grad, grads.at[y, :, pl.ds(0, HD)], local.at[1]
        )
        yield

    streams["A"] = attend_forward()
    streams["B"] = attend_backward()

    def having(name, stream):
        if name in held:
            arrive(held.pop(name))
        yield from stream

    half = sums[2][0].shape[3]
    own_terms, own_near = own
    query_part, kv_part = grads.at[:, :, pl.ds(0, HD)], grads.at[:, :, pl.ds(HD, HD)]
    own_pieces = [(grads.at[y, :, pl.ds(HD, HD)], full_kv), (handed, full_other)]
    streams["X"] = sum_kind(links, kv_terms.at[0], sums[0])
    streams["Y"] = sum_kind(links, kv_terms.at[1], sums[1])
    streams["h"] = hand_kv(links, sums[0][3], sums[1][3], cosine, sines, grads, handed)
    streams["u"] = own_groups(links, own_pieces, own_terms, own_near)
    streams["w"] = sum_weight(links, all_normed, kv_part, sums[8])
    for name, needs, stream in (
        ("a", "heads", sum_groups(links, all_heads, full_out, attn_out, 0, sums[2])),
        ("b", "heads", sum_groups(links, all_heads, full_out, attn_out, half, sums[3])),
        ("r", "grads", sum_groups(links, query_part, full_q, d_normed, 0, sums[4], own_terms)),
        ("s", "grads", sum_groups(links, query_part, full_q, d_normed, half, sums[5], own_terms)),
        ("f", "heads", sum_weight(links, all_d_out, all_heads, sums[6])),
        ("g", "grads", sum_weight(links, all_normed, query_part, sums[7])),
    ):
        streams[name] = having(needs, stream)
    in_order(streams, FRONT[9:] + BACK)
    to_end(streams)
    links.finish()
    placed_out, placed_q, placed_kv = sums[6][6], sums[7][6], sums[8][6]
    width = SIDE * HD
    for j in range(SIDE):
        d_w_out[:, j * HD : (j + 1) * HD] = placed_out[j]
        d_w_qkv[:, j * HD : (j + 1) * HD] = placed_q[j]
    for kind in range(2):
        total = placed_kv[kind].astype(jnp.float32) + placed_kv[kind + 2].astype(jnp.float32)
        d_w_qkv[:, width + kind * HD : width + (kind + 1) * HD] = total.astype(jnp.bfloat16)


def hand_on_kernel(*refs):
    half = len(refs) // 2
    for source, target in zip(refs[:half], refs[half:]):
        target[...] = source[...].reshape(target.shape)


VMEM = pl.BlockSpec(memory_space=pltpu.VMEM)
HBM = pl.BlockSpec(memory_space=pl.ANY)


def shape(*dims):
    return jax.ShapeDtypeStruct(dims, jnp.bfloat16)


def body(normed, w_qkv, w_out, block_order, d_out):
    rows, model = normed.shape[1], normed.shape[2]
    part = w_out.shape[0]
    length = rows * lax.axis_size("ctx")
    frequency = rope_base ** (-2.0 * np.arange(HD // 2, dtype=np.float64) / HD)
    frequency = np.tile(frequency, 2).astype(np.float32)[None, :]
    width = model // 4

    def vmem(*dims, kind=jnp.bfloat16):
        return pltpu.VMEM(dims, kind)

    blocks = vmem(4, rows, HD)
    copies = 5 * 10 + 2 * 8 + 1 + 2 * 7 + 4 * 3 + 2 * 9 + 1 + 2 + 4 * 9 + 3 * 12
    outs = [shape(rows, width), shape(rows, width), shape(*w_qkv.shape), shape(*w_out.shape)]
    results = pl.pallas_call(
        whole_kernel,
        out_shape=outs,
        in_specs=[HBM] * 4 + [pl.BlockSpec(memory_space=pltpu.SMEM), VMEM],
        out_specs=[VMEM] * 4,
        scratch_shapes=[
            (
                vmem(1, 2 * rows, kind=jnp.int32),
                vmem(length, 1, kind=jnp.int32),
                vmem(rows, HD, kind=jnp.float32),
                vmem(rows, HD, kind=jnp.float32),
            ),
            (vmem(4, rows, model),) * 2,
            (vmem(4, 4, 4, part, HD),) * 4,
            (blocks,) * 7,
            (vmem(4, rows, HD, kind=jnp.float32), vmem(4, rows, 2 * HD)),
            (
                vmem(2, rows, HD),
                vmem(2, 4, 4, rows, HD),
                vmem(2, length, HD, kind=jnp.float32),
                vmem(2, 4, 4, rows, HD),
                vmem(rows, HD),
                vmem(2, length, 2 * rows, kind=jnp.float32),
                vmem(2, 1, 2 * rows, kind=jnp.float32),
            ),
            (vmem(4, rows, width), vmem(2, rows, width)),
            (sum_kind_scratch(rows),) * 2
            + (sum_groups_scratch(rows, width // 2),) * 4
            + (sum_weight_scratch(part),) * 3,
            pltpu.SemaphoreType.DMA((copies,)),
            pltpu.SemaphoreType.DMA((copies,)),
            pltpu.SemaphoreType.DMA((6,)),
        ],
        compiler_params=pltpu.CompilerParams(
            collective_id=1, has_side_effects=True, vmem_limit_bytes=60 * 2**20
        ),
    )(
        normed,
        d_out,
        w_qkv,
        w_out,
        block_order,
        jnp.asarray(frequency),
    )
    outs = [shape(1, rows, width)] * 2 + outs[2:]
    return pl.pallas_call(hand_on_kernel, out_shape=outs)(*results)


def solution(mesh):
    in_specs = (
        P("dp", "ctx", None),
        P(("dp", "ctx"), "tp"),
        P(("dp", "ctx"), "tp"),
        P(),
        P("dp", "ctx", None),
    )
    out_specs = (
        P("dp", "ctx", "tp"),
        P("dp", "ctx", "tp"),
        P(("dp", "ctx"), "tp"),
        P(("dp", "ctx"), "tp"),
    )
    return jax.shard_map(body, mesh=mesh, in_specs=in_specs, out_specs=out_specs, check_vma=False)
```

```python
import jax
import jax.numpy as jnp
import numpy as np
from jax import lax
from jax.experimental import pallas as pl
from jax.experimental.pallas import tpu as pltpu
from jax.sharding import PartitionSpec as P

HD = 128
SIDE = 4
MESH = pl.DeviceIdType.MESH

rope_base = 500000.0
masked_score = -1e30
contract_last = (((1,), (1,)), ((), ()))
contract_first = (((0,), (0,)), ((), ()))


class Links:
    def __init__(self, send, recv):
        self.send, self.recv, self.used, self.copies = send, recv, 0, []
        self.y = lax.axis_index("dp")
        self.c = lax.axis_index("ctx")
        self.t = lax.axis_index("tp")
        self.x = self.c // SIDE
        self.z = self.c % SIDE
        self.core = lax.rem(self.t, 2)
        self.side = self.t // 2

    def along_y(self, k):
        return (lax.rem(self.y + k, SIDE), self.c, self.t)

    def along_x(self, k):
        return (self.y, lax.rem(self.x + k, SIDE) * SIDE + self.z, self.t)

    def along_z(self, k):
        return (self.y, self.x * SIDE + lax.rem(self.z + k, SIDE), self.t)

    def other_core(self):
        return (self.y, self.c, self.t + 1 - 2 * self.core)

    def other_side(self):
        return (self.y, self.c, lax.rem(self.t + 2, 4))

    def greet(self):
        partners = (
            [self.along_y(k) for k in (1, 2, 3)]
            + [self.along_z(k) for k in (1, 2, 3)]
            + [self.along_x(1), self.along_x(3), self.other_core(), self.other_side()]
        )
        barrier = pltpu.get_barrier_semaphore()
        for partner in partners:
            pl.semaphore_signal(barrier, inc=1, device_id=partner, device_id_type=MESH)
        pl.semaphore_wait(barrier, len(partners))

    def copy(self, source, target, partner):
        made = pltpu.make_async_remote_copy(
            src_ref=source,
            dst_ref=target,
            send_sem=self.send.at[self.used],
            recv_sem=self.recv.at[self.used],
            device_id=partner,
            device_id_type=MESH,
        )
        made.start()
        self.used += 1
        self.copies.append(made)
        return made

    def finish(self):
        for made in self.copies:
            made.wait_send()


def local_copy(source, target, semaphore):
    made = pltpu.make_async_copy(source, target, semaphore)
    made.start()
    return made


def in_order(streams, order):
    for name in order:
        next(streams[name], None)


def to_end(streams):
    for stream in streams.values():
        for _ in stream:
            pass


def column(i, width=HD):
    return pl.ds(pl.multiple_of(i * width, width), width)


def ring_gather(links, along, here, view, arrived=None):
    before, after, across = (
        lax.rem(here + 3, SIDE),
        lax.rem(here + 1, SIDE),
        lax.rem(here + 2, SIDE),
    )
    arrived = arrived or (lambda block: None)
    own = view(here, None)
    right = links.copy(own, own, along(1))
    left = links.copy(own, own, along(3))
    yield
    right.wait_recv()
    passed = view(before, 0)
    onward = links.copy(passed, passed, along(1))
    left.wait_recv()
    passed = view(after, 1)
    back = links.copy(passed, passed, along(3))
    arrived(view(before, None))
    arrived(view(after, None))
    yield
    onward.wait_recv()
    arrived(view(across, 0))
    back.wait_recv()
    arrived(view(across, 1))


def gather_columns(links, source, chosen, full, first=0, count=None, x_first=False):
    y, x, z = links.y, links.x, links.z
    rows = pl.ds(first, count or source.shape[0])
    place = full.at[y, x, z, rows]
    copies = [
        links.copy(
            source.at[rows, column(chosen(lax.rem(y + k, SIDE)))], place, links.along_y(k)
        )
        for k in (2, 1, 3)
    ]
    yield
    for made in copies:
        made.wait_recv()
    if x_first:
        yield from ring_gather(
            links,
            links.along_x,
            x,
            lambda i, h: full.at[:, i, z] if h is None else full.at[pl.ds(2 * h, 2), i, z],
        )
        block = full.at[:, :, z]
    else:
        block = full.at[:, x, z, rows]
    copies = [links.copy(block, block, links.along_z(k)) for k in (2, 1, 3)]
    yield
    for made in copies:
        made.wait_recv()
    if not x_first:
        yield from ring_gather(
            links,
            links.along_x,
            x,
            lambda i, h: full.at[:, i, :, rows]
            if h is None
            else full.at[pl.ds(2 * h, 2), i, :, rows],
        )


def gather_tokens(links, full, handed):
    half = full.shape[1] // 2
    first = pl.multiple_of(links.core * half, half)

    def view(i, h):
        if h is None:
            return full.at[i, pl.ds(first, half)]
        return full.at[i, pl.ds(pl.multiple_of(first + h * (half // 2), half // 2), half // 2)]

    def hand(block):
        handed.append(links.copy(block, block, links.other_core()))

    yield from ring_gather(links, links.along_y, links.y, view, hand)
    yield
    for made in handed[2:]:
        made.wait_recv()


def gather_kind(links, full):
    x, z = links.x, links.z
    block = full.at[x, z]
    copies = [links.copy(block, block, links.along_z(k)) for k in (2, 1, 3)]
    yield
    for made in copies:
        made.wait_recv()
    yield from ring_gather(
        links,
        links.along_x,
        x,
        lambda i, h: full.at[i] if h is None else full.at[i, pl.ds(2 * h, 2)],
    )


def exchange_heads(links, source, place, own_semaphore):
    copies = [
        links.copy(source.at[lax.rem(links.y + k, SIDE)], place, links.along_y(k))
        for k in (2, 1, 3)
    ]
    return copies, local_copy(source.at[links.y], place, own_semaphore)


def add_blocks(target, *terms):
    lead, (height, width) = target.shape[:-2], target.shape[-2:]
    rows = min(height, max(16, 16384 // width))
    per = height // rows
    count = per
    for size in lead:
        count *= size

    def step(i, carry):
        at = (pl.ds(pl.multiple_of(i % per * rows, rows), rows),)
        rest = i // per
        for size in lead[::-1]:
            at = (rest % size,) + at
            rest = rest // size
        total = terms[0][at].astype(jnp.float32)
        for term in terms[1:]:
            total = total + term[at].astype(jnp.float32)
        target[at] = total.astype(target.dtype)
        return carry

    lax.fori_loop(0, count, step, 0)


def ring_sum(links, along, here, view, result, scratch, prepare=None, extra=None, last=None):
    passing, from_left, from_right = scratch
    left, right, across = (
        lax.rem(here + 3, SIDE),
        lax.rem(here + 1, SIDE),
        lax.rem(here + 2, SIDE),
    )
    prepare = prepare or (lambda i: None)
    extra = extra or (lambda h: ())
    prepare(across)
    first = links.copy(view(across, 0), passing.at[0], along(1))
    second = links.copy(view(across, 1), passing.at[1], along(3))
    prepare(right)
    plain_right = links.copy(view(right, 1), from_left.at[1], along(1))
    prepare(left)
    plain_left = links.copy(view(left, 0), from_right.at[0], along(3))
    yield
    prepare(here)
    first.wait_recv()
    add_blocks(passing.at[0], passing.at[0], view(right, 0))
    summed_right = links.copy(passing.at[0], from_left.at[0], along(1))
    second.wait_recv()
    add_blocks(passing.at[1], passing.at[1], view(left, 1))
    summed_left = links.copy(passing.at[1], from_right.at[1], along(3))
    yield
    plain_left.wait_recv()
    summed_right.wait_recv()

    def parts(h):
        return (view(here, h), from_left.at[h], from_right.at[h]) + tuple(extra(h))

    if last is None:
        add_blocks(result(0), *parts(0))
    plain_right.wait_recv()
    summed_left.wait_recv()
    if last is None:
        add_blocks(result(1), *parts(1))
    else:
        last(parts)


def sum_weight(links, tokens, grads, scratch):
    terms, ring, middle, arrived, passed, summed, placed = scratch
    y, x, z = links.y, links.x, links.z
    size = 4 * terms.shape[3]

    def prepare(i):
        def step(owner, carry):
            at = column(owner * SIDE + i, size)
            rows = tokens[:, :, at].reshape(-1, size)
            part = lax.dot_general(
                rows,
                grads[...].reshape(rows.shape[0], HD),
                contract_first,
                preferred_element_type=jnp.float32,
            )
            terms[owner, i] = part.astype(jnp.bfloat16).reshape(terms.shape[2:])
            return carry

        lax.fori_loop(0, SIDE, step, 0)

    yield from ring_sum(
        links,
        links.along_x,
        x,
        lambda i, h: terms.at[pl.ds(2 * h, 2), i],
        lambda h: middle.at[pl.ds(2 * h, 2)],
        ring,
        prepare,
    )
    step = 1 + 2 * lax.rem(z, 2)
    neighbour, other = lax.rem(z + step, SIDE), lax.rem(z + 2, SIDE)
    first = links.copy(
        middle.at[:, lax.rem(neighbour + 2, SIDE)], arrived.at[0], links.along_z(step)
    )
    second = links.copy(middle.at[:, neighbour], arrived.at[1], links.along_z(step))
    yield
    first.wait_recv()
    add_blocks(passed, middle.at[:, other], arrived.at[0])
    third = links.copy(passed, arrived.at[2], links.along_z(2))
    yield
    second.wait_recv()
    third.wait_recv()
    add_blocks(summed, middle.at[:, z], arrived.at[1], arrived.at[2])
    copies = [
        links.copy(summed.at[lax.rem(y + k, SIDE)], placed.at[y], links.along_y(k))
        for k in (2, 1, 3)
    ]
    placed[y] = summed[y]
    yield
    for made in copies:
        made.wait_recv()


def sum_weight_scratch(rows):
    def vmem(*dims):
        return pltpu.VMEM(dims + (rows, HD), jnp.bfloat16)

    ring = (vmem(2, 2, 4), vmem(2, 2, 4), vmem(2, 2, 4))
    return (vmem(4, 4, 4), ring, vmem(4, 4), vmem(3, 4), vmem(4), vmem(4), vmem(4))


def sum_groups(links, rows, weight, result, start, scratch, own_part=None):
    terms, near, ring, paired, far = scratch
    whole, width = result.shape[1], terms.shape[3]
    core, side = links.core, links.side
    size = 256

    def prepare(owner):
        def step(i, carry):
            at = owner * (whole // size) + start // size + i
            part = lax.dot_general(
                rows[...].reshape(-1, HD),
                model_rows(weight, at, size),
                contract_last,
                preferred_element_type=jnp.float32,
            )
            terms[owner, :, :, column(i, size)] = part.astype(jnp.bfloat16).reshape(
                SIDE, rows.shape[1], size
            )
            return carry

        lax.fori_loop(0, width // size, step, 0)

    handed = []
    for i in range(2):
        prepare(2 * i + 1 - core)
        handed.append(links.copy(terms.at[2 * i + 1 - core], near.at[i], links.other_core()))
    for i in range(2):
        prepare(2 * i + core)
    yield
    for i in range(2):
        handed[i].wait_recv()
        add_blocks(terms.at[2 * i + core], terms.at[2 * i + core], near.at[i])
    sums = []

    def last(parts):
        add_blocks(paired, *parts(1 - side))
        sums.append(parts)

    yield from ring_sum(
        links,
        links.along_y,
        links.y,
        lambda i, h: terms.at[2 * h + core, i],
        None,
        ring,
        last=last,
        extra=None
        if own_part is None
        else lambda h: (own_part.at[2 * h + core, :, pl.ds(start, width)],),
    )
    across = links.copy(paired, far, links.other_side())
    yield
    across.wait_recv()
    add_blocks(result.at[:, pl.ds(start, width)], *sums[0](side), far)


def sum_groups_scratch(rows, width):
    def vmem(*dims):
        return pltpu.VMEM(dims + (rows, width), jnp.bfloat16)

    return (vmem(4, 4), vmem(2, 4), (vmem(2), vmem(2), vmem(2)), vmem(), vmem())


def model_rows(weight, i, size):
    return weight[i // 4, i % 4].reshape(size, HD)


def own_groups(links, pieces, terms, near):
    core = links.core
    width, size = terms.shape[2], 256

    def prepare(owner):
        def step(i, carry):
            at = owner * (width // size) + i
            part = sum(
                lax.dot_general(
                    rows[...],
                    model_rows(weight, at, size),
                    contract_last,
                    preferred_element_type=jnp.float32,
                )
                for rows, weight in pieces
            )
            terms[owner, :, column(i, size)] = part.astype(jnp.bfloat16)
            return carry

        lax.fori_loop(0, width // size, step, 0)

    handed = []
    for i in range(2):
        prepare(2 * i + 1 - core)
        handed.append(links.copy(terms.at[2 * i + 1 - core], near.at[i], links.other_core()))
    for i in range(2):
        prepare(2 * i + core)
    yield
    for i in range(2):
        handed[i].wait_recv()
        add_blocks(terms.at[2 * i + core], terms.at[2 * i + core], near.at[i])


def sum_kind(links, terms, scratch):
    ring, middle, arrived, total = scratch
    x, z = links.x, links.z
    yield from ring_sum(
        links,
        links.along_x,
        x,
        lambda i, h: terms.at[i, pl.ds(2 * h, 2)],
        lambda h: middle.at[pl.ds(2 * h, 2)],
        ring,
    )
    copies = [
        links.copy(middle.at[lax.rem(z + k, SIDE)], arrived.at[k - 1], links.along_z(k))
        for k in (2, 1, 3)
    ]
    yield
    for made in copies:
        made.wait_recv()
    add_blocks(total, middle.at[z], arrived.at[0], arrived.at[1], arrived.at[2])


def sum_kind_scratch(rows):
    def vmem(*dims):
        return pltpu.VMEM(dims + (rows, HD), jnp.bfloat16)

    return ((vmem(2, 2), vmem(2, 2), vmem(2, 2)), vmem(4), vmem(3), pltpu.VMEM((rows, HD), jnp.float32))


def arrive(exchange):
    copies, own = exchange
    for made in copies:
        made.wait_recv()
    own.wait()


def hand_kv(links, key_total, value_total, cosine, sines, grads, handed):
    y = links.y
    key, value = key_total[...], value_total[...]
    key = key * cosine[...] - pltpu.roll(key, HD // 2, 1) * sines[...]
    keeps_key = lax.rem(y, 2) == 0
    handed[...] = jnp.where(keeps_key, value, key).astype(jnp.bfloat16)
    passed = links.copy(handed, grads.at[y, :, pl.ds(HD, HD)], links.along_y(3))
    grads[y, :, HD:] = jnp.where(keeps_key, key, value).astype(jnp.bfloat16)
    yield
    passed.wait_recv()


def project(sequences, weight, target):
    size = 1024

    def step(i, carry):
        part = jnp.dot(
            jnp.concatenate([tokens[:, column(i, size)] for tokens in sequences]),
            weight[i].reshape(size, HD),
            preferred_element_type=jnp.float32,
        ).reshape(target.shape)
        target[...] = jnp.where(i == 0, part, target[...] + part)
        return carry

    lax.fori_loop(0, SIDE, step, 0)


def attend(query_pos, key_pos, queries, kv, heads_out, raws, row_sums):
    to_power = HD ** (-0.5) * float(np.log2(np.e))
    length = key_pos.shape[0]
    pair = 2
    rows = pair * queries.shape[1]
    keys = kv[0].reshape(length, HD)
    values_t = kv[1].reshape(length, HD).T

    def step(i, carry):
        at = pl.ds(i * pair, pair)
        q = queries[at].reshape(rows, HD)
        allowed = key_pos[...] <= query_pos[...]
        scores = lax.dot_general(keys, q, contract_last, preferred_element_type=jnp.float32)
        scores = jnp.where(allowed, scores, masked_score)
        row_max = jnp.max(scores, axis=0, keepdims=True)
        raw = jnp.exp2((scores - row_max) * to_power)
        raws[i] = raw
        row_sum = jnp.sum(raw, axis=0, keepdims=True)
        row_sums[i] = row_sum
        weighted = jnp.dot(values_t, raw.astype(jnp.bfloat16), preferred_element_type=jnp.float32)
        heads_out[at] = (weighted / row_sum).T.astype(jnp.bfloat16).reshape(pair, -1, HD)
        return carry

    lax.fori_loop(0, queries.shape[0] // pair, step, 0)


def attend_back(
    i, cosine, sines, queries, head_grads, kv, heads_out, raws, row_sums, query_grad, totals
):
    score_scale = HD ** (-0.5)
    length = raws.shape[1]
    pair = 2
    rows = pair * queries.shape[1]
    keys_t = kv[0].reshape(length, HD).T
    values = kv[1].reshape(length, HD)
    turn = jnp.concatenate([cosine[...]] * pair), jnp.concatenate([sines[...]] * pair)
    at = pl.ds(i * pair, pair)
    q, grads = queries[at].reshape(rows, HD), head_grads[at].reshape(rows, HD)
    out = heads_out[at].reshape(rows, HD)
    row_dots = jnp.sum(
        (grads.astype(jnp.float32) * out.astype(jnp.float32)).T, axis=0, keepdims=True
    )
    weights = raws[i] * (1.0 / row_sums[i])
    dweights = lax.dot_general(values, grads, contract_last, preferred_element_type=jnp.float32)
    dscores = (weights * (dweights - row_dots)).astype(jnp.bfloat16)
    dq = jnp.dot(keys_t, dscores, preferred_element_type=jnp.float32).T * score_scale
    dq = dq * turn[0] - pltpu.roll(dq, HD // 2, 1) * turn[1]
    query_grad[at] = dq.astype(jnp.bfloat16).reshape(pair, -1, HD)
    key_part = jnp.dot(dscores, q, preferred_element_type=jnp.float32) * score_scale
    value_part = jnp.dot(
        weights.astype(jnp.bfloat16), grads, preferred_element_type=jnp.float32
    )
    totals[0] = key_part if i == 0 else totals[0] + key_part
    totals[1] = value_part if i == 0 else totals[1] + value_part


def place_tables(links, order, frequency, query_pos, key_pos, cosine, sines):
    rows = cosine.shape[0]
    block = rows // 2
    first, second = order[2 * links.c] * block, order[2 * links.c + 1] * block

    def positions(dims, axis):
        row = lax.rem(lax.broadcasted_iota(jnp.int32, dims, axis), rows)
        return jnp.where(row < block, first, second - block) + row

    query_pos[...] = positions(query_pos.shape, 1)
    angles = positions(cosine.shape, 0).astype(jnp.float32) * frequency[...]
    lane = lax.broadcasted_iota(jnp.int32, sines.shape, 1)
    sine = jnp.sin(angles)
    cosine[...] = jnp.cos(angles)
    sines[...] = jnp.where(lane < HD // 2, -sine, sine)
    row = lax.broadcasted_iota(jnp.int32, (block, 1), 0)
    for i in range(key_pos.shape[0] // block):
        key_pos[i * block : (i + 1) * block] = order[i] * block + row


FRONT = "kqojnkdjokjjkqonjkPqovdqPKvVnKqVvnQdKVovdGKV"
BACK = "ABBXYbabXYgbYXagrbvfaYXhgrfuahwsfrwugsafwgrsbwsrwgfsfw"


def whole_kernel(
    normed, d_out, w_qkv, w_out, order, frequency,
    attn_out, d_normed, d_w_qkv, d_w_out,
    tables, tokens, weights, blocks, wide, rows_kv, own, sums, send, recv, local,
):
    links = Links(send, recv)
    y, x, z = links.y, links.x, links.z
    heads = w_out.shape[1] // HD
    query_pos, key_pos, cosine, sines = tables
    all_normed, all_d_out = tokens
    full_q, full_kv, full_out, full_other = weights
    my_queries, my_grads, queries, head_grads, heads_out, query_grad, all_heads = blocks
    projected, grads = wide
    my_kv, all_kv, totals, kv_terms, handed, raws, row_sums = rows_kv
    after = lax.rem(y + 1, SIDE)

    given = {
        "k": (w_qkv, lambda j: heads + lax.rem(j, 2), full_kv),
        "q": (w_qkv, lambda j: j, full_q),
        "o": (w_out, lambda j: j, full_out),
        "v": (w_qkv, lambda j: heads + lax.rem(j + 1, 2), full_other),
    }
    mine = [
        local_copy(source.at[:, column(chosen(y))], full.at[y, x, z], local.at[i])
        for i, (source, chosen, full) in enumerate(given.values())
    ]
    mine += [
        local_copy(source.at[0], full.at[y], local.at[4 + i])
        for i, (source, full) in enumerate(((normed, all_normed), (d_out, all_d_out)))
    ]
    for k in (2, 3):
        grads[lax.rem(y + k, SIDE), :, HD:] = jnp.zeros_like(grads[0, :, HD:])
    links.greet()
    streams = {name: gather_columns(links, *given[name]) for name in "qo"}
    half = w_qkv.shape[0] // 2
    streams["k"] = gather_columns(links, *given["k"], 0, half)
    streams["j"] = gather_columns(links, *given["k"], half, half)
    streams["v"] = gather_columns(links, *given["v"], x_first=True)
    handed_n, handed_d = [], []
    streams["n"] = gather_tokens(links, all_normed, handed_n)
    streams["d"] = gather_tokens(links, all_d_out, handed_d)
    for made in mine:
        made.wait()
    in_order(streams, FRONT[:9])
    place_tables(links, order, frequency, query_pos, key_pos, cosine, sines)
    held = {}

    def project_kv():
        for made in handed_n[:2]:
            made.wait_recv()
        project([all_normed.at[y], all_normed.at[after]], full_kv, projected.at[pl.ds(0, 2)])
        for i in range(2):
            part = projected[i]
            turned = part * cosine[...] + pltpu.roll(part, HD // 2, 1) * sines[...]
            my_kv[i] = jnp.where(lax.rem(y, 2) == 0, turned, part).astype(jnp.bfloat16)
        place = all_kv.at[lax.rem(y, 2), x, z]
        passed = links.copy(my_kv.at[1], place, links.along_y(1))
        place[...] = my_kv[0]
        yield
        passed.wait_recv()

    def project_queries():
        project([all_normed.at[i] for i in range(SIDE)], full_q, projected)
        for i in range(SIDE):
            part = projected[i]
            turned = part * cosine[...] + pltpu.roll(part, HD // 2, 1) * sines[...]
            my_queries[i] = turned.astype(jnp.bfloat16)
        held["Q"] = exchange_heads(links, my_queries, queries.at[y], local.at[0])
        yield

    def project_grads():
        for made in handed_d[:2]:
            made.wait_recv()
        project([all_d_out.at[i] for i in range(SIDE)], full_out, projected)
        my_grads[...] = projected[...].astype(jnp.bfloat16)
        held["G"] = exchange_heads(links, my_grads, head_grads.at[y], local.at[1])
        yield

    streams["P"] = project_kv()
    streams["Q"] = project_queries()
    streams["G"] = project_grads()
    streams["K"] = gather_kind(links, all_kv.at[0])
    streams["V"] = gather_kind(links, all_kv.at[1])

    def attend_forward():
        arrive(held.pop("Q"))
        attend(query_pos, key_pos, queries, all_kv, heads_out, raws, row_sums)
        held["heads"] = exchange_heads(links, heads_out, all_heads.at[y], local.at[0])
        yield

    def attend_backward():
        arrive(held.pop("G"))
        for i in range(2):
            attend_back(
                i, cosine, sines, queries, head_grads, all_kv, heads_out, raws, row_sums,
                query_grad, totals,
            )
            if i == 0:
                yield
        kv_terms[...] = totals[...].astype(jnp.bfloat16).reshape(kv_terms.shape)
        held["grads"] = exchange_heads(
            links, query_grad, grads.at[y, :, pl.ds(0, HD)], local.at[1]
        )
        yield

    streams["A"] = attend_forward()
    streams["B"] = attend_backward()

    def having(name, stream):
        if name in held:
            arrive(held.pop(name))
        yield from stream

    half = sums[2][0].shape[3]
    own_terms, own_near = own
    query_part, kv_part = grads.at[:, :, pl.ds(0, HD)], grads.at[:, :, pl.ds(HD, HD)]
    own_pieces = [(grads.at[y, :, pl.ds(HD, HD)], full_kv), (handed, full_other)]
    streams["X"] = sum_kind(links, kv_terms.at[0], sums[0])
    streams["Y"] = sum_kind(links, kv_terms.at[1], sums[1])
    streams["h"] = hand_kv(links, sums[0][3], sums[1][3], cosine, sines, grads, handed)
    streams["u"] = own_groups(links, own_pieces, own_terms, own_near)
    streams["w"] = sum_weight(links, all_normed, kv_part, sums[8])
    for name, needs, stream in (
        ("a", "heads", sum_groups(links, all_heads, full_out, attn_out, 0, sums[2])),
        ("b", "heads", sum_groups(links, all_heads, full_out, attn_out, half, sums[3])),
        ("r", "grads", sum_groups(links, query_part, full_q, d_normed, 0, sums[4], own_terms)),
        ("s", "grads", sum_groups(links, query_part, full_q, d_normed, half, sums[5], own_terms)),
        ("f", "heads", sum_weight(links, all_d_out, all_heads, sums[6])),
        ("g", "grads", sum_weight(links, all_normed, query_part, sums[7])),
    ):
        streams[name] = having(needs, stream)
    in_order(streams, FRONT[9:] + BACK)
    to_end(streams)
    links.finish()
    placed_out, placed_q, placed_kv = sums[6][6], sums[7][6], sums[8][6]
    width = SIDE * HD
    for j in range(SIDE):
        d_w_out[:, j * HD : (j + 1) * HD] = placed_out[j]
        d_w_qkv[:, j * HD : (j + 1) * HD] = placed_q[j]
    for kind in range(2):
        total = placed_kv[kind].astype(jnp.float32) + placed_kv[kind + 2].astype(jnp.float32)
        d_w_qkv[:, width + kind * HD : width + (kind + 1) * HD] = total.astype(jnp.bfloat16)


def hand_on_kernel(*refs):
    half = len(refs) // 2
    for source, target in zip(refs[:half], refs[half:]):
        target[...] = source[...].reshape(target.shape)


VMEM = pl.BlockSpec(memory_space=pltpu.VMEM)
HBM = pl.BlockSpec(memory_space=pl.ANY)


def shape(*dims):
    return jax.ShapeDtypeStruct(dims, jnp.bfloat16)


def body(normed, w_qkv, w_out, block_order, d_out):
    rows, model = normed.shape[1], normed.shape[2]
    part = w_out.shape[0]
    length = rows * lax.axis_size("ctx")
    frequency = rope_base ** (-2.0 * np.arange(HD // 2, dtype=np.float64) / HD)
    frequency = np.tile(frequency, 2).astype(np.float32)[None, :]
    width = model // 4

    def vmem(*dims, kind=jnp.bfloat16):
        return pltpu.VMEM(dims, kind)

    blocks = vmem(4, rows, HD)
    copies = 5 * 10 + 2 * 8 + 1 + 2 * 7 + 4 * 3 + 2 * 9 + 1 + 2 + 4 * 9 + 3 * 12
    outs = [shape(rows, width), shape(rows, width), shape(*w_qkv.shape), shape(*w_out.shape)]
    results = pl.pallas_call(
        whole_kernel,
        out_shape=outs,
        in_specs=[HBM] * 4 + [pl.BlockSpec(memory_space=pltpu.SMEM), VMEM],
        out_specs=[VMEM] * 4,
        scratch_shapes=[
            (
                vmem(1, 2 * rows, kind=jnp.int32),
                vmem(length, 1, kind=jnp.int32),
                vmem(rows, HD, kind=jnp.float32),
                vmem(rows, HD, kind=jnp.float32),
            ),
            (vmem(4, rows, model),) * 2,
            (vmem(4, 4, 4, part, HD),) * 4,
            (blocks,) * 7,
            (vmem(4, rows, HD, kind=jnp.float32), vmem(4, rows, 2 * HD)),
            (
                vmem(2, rows, HD),
                vmem(2, 4, 4, rows, HD),
                vmem(2, length, HD, kind=jnp.float32),
                vmem(2, 4, 4, rows, HD),
                vmem(rows, HD),
                vmem(2, length, 2 * rows, kind=jnp.float32),
                vmem(2, 1, 2 * rows, kind=jnp.float32),
            ),
            (vmem(4, rows, width), vmem(2, rows, width)),
            (sum_kind_scratch(rows),) * 2
            + (sum_groups_scratch(rows, width // 2),) * 4
            + (sum_weight_scratch(part),) * 3,
            pltpu.SemaphoreType.DMA((copies,)),
            pltpu.SemaphoreType.DMA((copies,)),
            pltpu.SemaphoreType.DMA((6,)),
        ],
        compiler_params=pltpu.CompilerParams(
            collective_id=1, has_side_effects=True, vmem_limit_bytes=60 * 2**20
        ),
    )(
        normed,
        d_out,
        w_qkv,
        w_out,
        block_order,
        jnp.asarray(frequency),
    )
    outs = [shape(1, rows, width)] * 2 + outs[2:]
    return pl.pallas_call(hand_on_kernel, out_shape=outs)(*results)


def solution(mesh):
    in_specs = (
        P("dp", "ctx", None),
        P(("dp", "ctx"), "tp"),
        P(("dp", "ctx"), "tp"),
        P(),
        P("dp", "ctx", None),
    )
    out_specs = (
        P("dp", "ctx", "tp"),
        P("dp", "ctx", "tp"),
        P(("dp", "ctx"), "tp"),
        P(("dp", "ctx"), "tp"),
    )
    return jax.shard_map(body, mesh=mesh, in_specs=in_specs, out_specs=out_specs, check_vma=False)
```
